128 devices in a mesh: ha: 8 (over z, x_lo), wa: 4 (over y), ta: 4 (over x_hi, core).
Axes of the slice: x: 4 (x_hi: 2, x_lo: 2; x = x_hi * 2 + x_lo), y: 4, z: 4, core: 2. Of those that a mesh axis runs over, the one named last changes fastest.
Arguments:
- queries: bfloat16 [12, 32, 64, 3072], P(None, 'wa', 'ha', 'ta'), may hold values from -10 to 10, as said below
- keys_values: bfloat16 [2, 12, 32, 64, 3072], P(None, None, 'wa', 'ha', 'ta'), may hold values from -6 to 6
- out_weight: bfloat16 [3072, 3072], P('ta'), may hold values from -2.5 to 2.5
Outputs:
- projected: bfloat16 [12, 32, 64, 3072], P(None, 'wa', 'ha', 'ta')
The draws below stay inside these ranges and needn't reach their ends.
Inputs may be any that keep to these rules, and one draw needn't show every extreme that they name: `queries`: query entries.
All inputs are finite; a program needn't handle non-finite values.
Results may differ from the reference program's by a relative error of at most 0.013.
Values may be sent and summed in bfloat16 or wider, within the bound.
No kernel may reach another device: no remote copies, remote signals or barrier semaphores. Data moves between devices by JAX's collectives and lax.ppermute only.
A program may use at most 128 MiB of HBM per device.

```python
import jax
import jax.numpy as jnp
from jax import lax

D = 3072
HEADS = 24
HD = 128
FRAMES = 12
TILE_T = 6
TILE_H = 8
TILE_W = 8
NH = 32
NW = 64
N_TA = 4


def draw_queries(key, part):
    key = jax.random.fold_in(key, 7)
    shape = (FRAMES, NH, NW, HEADS * HD)
    result = jnp.clip(jax.random.normal(key, shape, jnp.float32), -6.0, 6.0)
    return result.astype(jnp.bfloat16)


def draw_keys_values(key, part):
    key = jax.random.fold_in(key, 13)
    shape = (FRAMES, NH, NW, HEADS * HD)
    first_key = jax.random.fold_in(key, 0)
    third_key = jax.random.fold_in(key, 2)
    values = jnp.clip(jax.random.normal(third_key, shape, jnp.float32), -6.0, 6.0)
    keys = jnp.clip(jax.random.normal(first_key, shape, jnp.float32), -6.0, 6.0)
    return jnp.stack([keys, values]).astype(jnp.bfloat16)


def levels(rng, extent, pieces, low, high):
    def one(position, blocks):
        heights = jax.random.uniform(jax.random.fold_in(jax.random.fold_in(rng, 6), position), (blocks,), jnp.float32, low / len(pieces), high / len(pieces))
        return jnp.repeat(jnp.exp(heights), extent[position] // blocks).reshape((-1,) + (1,) * (len(extent) - position - 1))

    factor_of = one(*pieces[0])
    for cut in pieces[1:]:
        factor_of = factor_of * one(*cut)
    return factor_of


def scatter_about(rng, extent, width, bound, cuts=(), held_as=jnp.bfloat16):
    array = jax.random.normal(rng, extent, jnp.float32) * width
    if len(cuts) > 0:
        array = levels(rng, extent, cuts, -0.22, 0.18) * array
    return jnp.clip(array, min=-bound, max=bound).astype(held_as)


def setup_inputs(seed: int = 0) -> dict:
    seeds = jax.random.split(jax.random.key(seed), 4)
    queries = draw_queries(jax.random.fold_in(seeds[3], 71), 0)
    keys_values = draw_keys_values(jax.random.fold_in(seeds[3], 71), 0)
    out_weight = scatter_about(seeds[2], (HEADS * HD, D), (max(D // 512, 1)) ** -0.5, 2.5, ((0, 4),))
    return dict(queries=queries, keys_values=keys_values, out_weight=out_weight)


def attend_tile(tile_queries, tile_keys, tile_values, allowed):
    scores = jnp.einsum("qhd,khd->hqk", tile_queries, tile_keys) * (HD ** -0.5)
    scores = jnp.where(allowed, scores, -1e30)
    row_max = jnp.max(scores, axis=2, keepdims=True)
    weights = jnp.where(allowed, jnp.exp(scores - row_max), 0.0)
    row_total = jnp.sum(weights, axis=2)
    rounded = lax.optimization_barrier(weights.astype(jnp.bfloat16)).astype(jnp.float32)
    attended = jnp.einsum("hqk,khd->qhd", rounded, tile_values)
    return attended / jnp.transpose(row_total)[:, :, None]


def reference(queries, keys_values, out_weight):
    row_tiles = NH // TILE_H
    col_tiles = NW // TILE_W
    channels = HEADS * HD
    padded = jnp.pad(keys_values, ((0, 0), (0, 0), (TILE_H, TILE_H), (TILE_W, TILE_W), (0, 0)))
    frame_ids = jnp.arange(FRAMES, dtype=jnp.int32)
    query_frames = jnp.broadcast_to(frame_ids[:, None, None], (FRAMES, TILE_H, TILE_W)).reshape(-1)
    key_frames = jnp.broadcast_to(frame_ids[:, None, None], (FRAMES, 3 * TILE_H, 3 * TILE_W)).reshape(-1)
    frame_near = jnp.abs(query_frames[:, None] // TILE_T - key_frames[None, :] // TILE_T) <= 1

    def one_tile(tile_index):
        row_tile = tile_index // col_tiles
        col_tile = tile_index % col_tiles
        start_row = (row_tile * TILE_H).astype(jnp.int32)
        start_col = (col_tile * TILE_W).astype(jnp.int32)
        zero = jnp.int32(0)
        tile_queries = lax.dynamic_slice(queries, (zero, start_row, start_col, zero), (FRAMES, TILE_H, TILE_W, channels))
        tile_pairs = lax.dynamic_slice(padded, (zero, zero, start_row, start_col, zero), (2, FRAMES, 3 * TILE_H, 3 * TILE_W, channels))
        key_rows = start_row - TILE_H + jnp.arange(3 * TILE_H, dtype=jnp.int32)
        key_cols = start_col - TILE_W + jnp.arange(3 * TILE_W, dtype=jnp.int32)
        inside = ((key_rows >= 0) & (key_rows < NH))[:, None] & ((key_cols >= 0) & (key_cols < NW))[None, :]
        inside = jnp.broadcast_to(inside[None], (FRAMES, 3 * TILE_H, 3 * TILE_W)).reshape(-1)
        allowed = (frame_near & inside[None, :])[None]
        attended = attend_tile(
            tile_queries.astype(jnp.float32).reshape(-1, HEADS, HD),
            tile_pairs[0].astype(jnp.float32).reshape(-1, HEADS, HD),
            tile_pairs[1].astype(jnp.float32).reshape(-1, HEADS, HD),
            allowed)
        return attended.astype(jnp.bfloat16).reshape(FRAMES, TILE_H, TILE_W, channels)

    tile_outputs = lax.map(one_tile, jnp.arange(row_tiles * col_tiles, dtype=jnp.int32))
    attention = tile_outputs.reshape(row_tiles, col_tiles, FRAMES, TILE_H, TILE_W, channels)
    attention = attention.transpose(2, 0, 3, 1, 4, 5).reshape(FRAMES * NH * NW, channels)
    group_width = channels // N_TA
    summed = jnp.zeros((FRAMES * NH * NW, D), jnp.float32)
    for member in range(N_TA):
        part_sum = jnp.dot(attention[:, member * group_width:(member + 1) * group_width],
                           out_weight[member * group_width:(member + 1) * group_width],
                           preferred_element_type=jnp.float32)
        summed = summed + part_sum.astype(jnp.bfloat16).astype(jnp.float32)
    return summed.astype(jnp.bfloat16).reshape(FRAMES, NH, NW, D)
```

```python
import functools

import jax
import jax.numpy as jnp
from jax import lax
from jax.experimental import pallas as pl
from jax.experimental.pallas import tpu as pltpu
from jax.sharding import PartitionSpec as P

HD = 128
LOG2E = 1.4426950408889634
EXP_SCALE = HD ** (-0.5) * LOG2E
BQ = 256
LOW = -1e30


def attend_kernel(gates, first, last, *refs):
    flags_ref, q_ref = refs[:2]
    tiles = refs[2 : 2 + len(gates)]
    rest = refs[2 + len(gates) :]
    if not first:
        acc_in, top_in = rest[:2]
        rest = rest[2:]
    tokens = q_ref.shape[0]
    span = tiles[0].shape[1]
    inside = [None if gate is None else flags_ref[gate] > 0 for gate in gates]

    def scores_of(start):
        queries = q_ref[pl.ds(start, BQ), :]
        return [
            lax.dot_general(
                queries, tile[0], (((1,), (1,)), ((), ())), preferred_element_type=jnp.float32
            )
            for tile in tiles
        ]

    def finish(start, scores):
        rows = pl.ds(start, BQ)
        old = jnp.full((BQ, HD), LOW, jnp.float32) if first else top_in[rows, :]
        new = old
        for score, valid in zip(scores, inside):
            largest = jnp.broadcast_to(jnp.max(score, axis=1, keepdims=True), (BQ, HD))
            if valid is not None:
                largest = jnp.where(valid, largest, LOW)
            new = jnp.maximum(new, largest)
        mixed = None
        for score, valid, tile in zip(scores, inside, tiles):
            shift = new if valid is None else jnp.where(valid, new, -LOW)
            wide = jnp.concatenate([shift] * (span // HD), axis=1)
            weights = jnp.exp2((score - wide) * EXP_SCALE).astype(jnp.bfloat16)
            values = jnp.concatenate([tile[1], jnp.ones((span, HD), jnp.bfloat16)], axis=1)
            part = jnp.dot(weights, values, preferred_element_type=jnp.float32)
            mixed = part if mixed is None else mixed + part
        if not first:
            keep = jnp.exp2((old - new) * EXP_SCALE)
            mixed = acc_in[rows, :] * jnp.concatenate([keep, keep], axis=1) + mixed
        if last:
            rest[0][rows, :] = (mixed[:, :HD] / mixed[:, HD:]).astype(rest[0].dtype)
        else:
            rest[0][rows, :] = mixed
            rest[1][rows, :] = new

    scores = scores_of(0)
    for start in range(0, tokens, BQ):
        following = scores_of(start + BQ) if start + BQ < tokens else None
        finish(start, scores)
        scores = following


def attend(flags, queries, tiles, gates, state=None, last=False):
    tokens, channels = queries.shape
    heads = channels // HD
    span = tiles[0].shape[1]
    q_spec = pl.BlockSpec((tokens, HD), lambda h: (0, h))
    acc_spec = pl.BlockSpec((tokens, 2 * HD), lambda h: (0, h))
    tile_spec = pl.BlockSpec((2, span, HD), lambda h: (0, 0, h))
    in_specs = [pl.BlockSpec(memory_space=pltpu.SMEM), q_spec] + [tile_spec] * len(tiles)
    args = [flags, queries, *tiles]
    if state is not None:
        in_specs += [acc_spec, q_spec]
        args += list(state)
    if last:
        out_shape = jax.ShapeDtypeStruct((tokens, channels), jnp.bfloat16)
        out_specs = q_spec
    else:
        out_shape = [
            jax.ShapeDtypeStruct((tokens, 2 * channels), jnp.float32),
            jax.ShapeDtypeStruct((tokens, channels), jnp.float32),
        ]
        out_specs = [acc_spec, q_spec]
    pairs = len(tiles) * heads * tokens * span
    return pl.pallas_call(
        functools.partial(attend_kernel, tuple(gates), state is None, last),
        out_shape=out_shape,
        grid=(heads,),
        in_specs=in_specs,
        out_specs=out_specs,
        compiler_params=pltpu.CompilerParams(vmem_limit_bytes=48 * 1024 * 1024),
        cost_estimate=pl.CostEstimate(
            flops=pairs * 8 * HD, bytes_accessed=len(tiles) * span * channels * 4, transcendentals=pairs
        ),
    )(*args)


def after(value, *others):
    return lax.optimization_barrier((value, *others))[0]


def body(queries, keys_values, out_weight):
    frames, rows, cols, channels = queries.shape
    tokens = frames * rows * cols
    half = channels // 2
    ha_count, wa_count = lax.axis_size("ha"), lax.axis_size("wa")
    ha, wa, ta = lax.axis_index("ha"), lax.axis_index("wa"), lax.axis_index("ta")
    odd = lax.rem(ha, 2)

    q_all = queries.reshape(tokens, channels)
    kv_all = keys_values.reshape(2, tokens, channels)
    keep_at, send_at = odd * half, (1 - odd) * half

    swap_pairs = [(i, i ^ 1) for i in range(ha_count)]
    native_pairs = [(i, (i + (2 if i % 2 else -2)) % ha_count) for i in range(ha_count)]
    swapped_pairs = [(i, (i + (-2 if i % 2 else 2)) % ha_count) for i in range(ha_count)]
    down_pairs = [(i, (i + 1) % wa_count) for i in range(wa_count)]
    up_pairs = [((i + 1) % wa_count, i) for i in range(wa_count)]

    def above_below(cells):
        return lax.ppermute(cells, "wa", down_pairs), lax.ppermute(cells, "wa", up_pairs)

    above, below = wa > 0, wa < wa_count - 1
    low, high = ha >= 2, ha < ha_count - 2
    far_partner = jnp.where(odd == 1, low, high)
    far_native = jnp.where(odd == 1, high, low)
    flags = jnp.stack(
        [above, below, far_partner, far_partner & above, far_partner & below,
         far_native, far_native & above, far_native & below]
    ).astype(jnp.int32)

    kv_send = lax.dynamic_slice_in_dim(kv_all, send_at, half, 2)
    kv_own = lax.dynamic_slice_in_dim(kv_all, keep_at, half, 2)
    q_send = lax.dynamic_slice_in_dim(q_all, send_at, half, 1)
    q_own = lax.dynamic_slice_in_dim(q_all, keep_at, half, 1)

    kv_pair = lax.ppermute(kv_send, "ha", swap_pairs)
    own_up, own_down = above_below(kv_own)
    far_p = lax.ppermute(kv_own, "ha", native_pairs)
    q_pair = lax.ppermute(after(q_send, kv_pair), "ha", swap_pairs)
    pair_up, pair_down = above_below(kv_pair)
    far_n = lax.ppermute(kv_pair, "ha", swapped_pairs)
    far_p_up = lax.ppermute(own_up, "ha", native_pairs)
    far_p_down = lax.ppermute(own_down, "ha", native_pairs)
    far_n_up, far_n_down = above_below(far_n)

    state_n = attend(flags, q_own, [kv_own], [None])
    state_n = attend(flags, q_own, [kv_pair, own_up, own_down], [None, 0, 1], state_n)
    state_p = attend(flags, q_pair, [kv_own, kv_pair, own_up, own_down, far_p], [None, None, 0, 1, 2])
    state_p = attend(flags, q_pair, [pair_up, pair_down], [0, 1], state_p)
    state_n = attend(flags, q_own, [pair_up, pair_down, far_n], [0, 1, 5], state_n)
    out_p = attend(flags, q_pair, [far_p_up, far_p_down], [3, 4], state_p, last=True)
    back = lax.ppermute(out_p, "ha", swap_pairs)
    out_n = attend(flags, q_own, [far_n_up, far_n_down], [6, 7], state_n, last=True)

    core, x_hi = lax.rem(ta, 2), ta // 2
    width = out_weight.shape[1] // lax.axis_size("ta")
    weight_n = lax.dynamic_slice_in_dim(out_weight, keep_at, half, 0)
    weight_p = lax.dynamic_slice_in_dim(out_weight, send_at, half, 0)
    attention = jnp.concatenate([out_n, back], axis=1)
    weight = jnp.concatenate([weight_n, weight_p], axis=0)

    def partial_of(group):
        columns = lax.dynamic_slice_in_dim(weight, group * width, width, 1)
        return jnp.dot(attention, columns, preferred_element_type=jnp.float32)

    core_pairs = [(i, i ^ 1) for i in range(4)]
    hi_pairs = [(i, i ^ 2) for i in range(4)]
    away_other = partial_of(2 * (1 - x_hi) + 1 - core).astype(jnp.bfloat16)
    away_in = lax.ppermute(away_other, "ta", core_pairs)
    away = (partial_of(2 * (1 - x_hi) + core) + away_in.astype(jnp.float32)).astype(jnp.bfloat16)
    home_far = lax.ppermute(away, "ta", hi_pairs)
    home_other = partial_of(2 * x_hi + 1 - core).astype(jnp.bfloat16)
    home_in = lax.ppermute(home_other, "ta", core_pairs)
    home = partial_of(ta) + home_in.astype(jnp.float32) + home_far.astype(jnp.float32)
    return home.astype(jnp.bfloat16).reshape(frames, rows, cols, width)


def solution(mesh):
    return jax.shard_map(
        body,
        mesh=mesh,
        in_specs=(P(None, "wa", "ha", "ta"), P(None, None, "wa", "ha", "ta"), P("ta", None)),
        out_specs=P(None, "wa", "ha", "ta"),
        check_vma=False,
    )
```

```python
import functools

import jax
import jax.numpy as jnp
from jax import lax
from jax.experimental import pallas as pl
from jax.experimental.pallas import tpu as pltpu
from jax.sharding import PartitionSpec as P

HD = 128
LOG2E = 1.4426950408889634
EXP_SCALE = HD ** (-0.5) * LOG2E
LOW = -1e30


COST2 = 1024


def attend_kernel(gates, first, last, step, *refs):
    flags_ref, q_ref = refs[:2]
    tiles = refs[2 : 2 + len(gates)]
    rest = refs[2 + len(gates) :]
    if not first:
        acc_in, top_in = rest[:2]
        rest = rest[2:]
    tokens = q_ref.shape[0]
    span = tiles[0].shape[1]
    inside = [None if gate is None else flags_ref[gate] > 0 for gate in gates]

    def scores_of(start):
        queries = q_ref[pl.ds(start, step), :]
        return [
            lax.dot_general(
                queries, tile[0], (((1,), (1,)), ((), ())), preferred_element_type=jnp.float32
            )
            for tile in tiles
        ]

    def finish(start, scores):
        rows = pl.ds(start, step)
        old = jnp.full((step, HD), LOW, jnp.float32) if first else top_in[rows, :]
        new = old
        for score, valid in zip(scores, inside):
            largest = jnp.broadcast_to(jnp.max(score, axis=1, keepdims=True), (step, HD))
            if valid is not None:
                largest = jnp.where(valid, largest, LOW)
            new = jnp.maximum(new, largest)
        mixed = None
        for score, valid, tile in zip(scores, inside, tiles):
            shift = new if valid is None else jnp.where(valid, new, -LOW)
            wide = jnp.concatenate([shift] * (span // HD), axis=1)
            weights = jnp.exp2((score - wide) * EXP_SCALE).astype(jnp.bfloat16)
            values = jnp.concatenate([tile[1], jnp.ones((span, HD), jnp.bfloat16)], axis=1)
            part = jnp.dot(weights, values, preferred_element_type=jnp.float32)
            mixed = part if mixed is None else mixed + part
        if not first:
            keep = jnp.exp2((old - new) * EXP_SCALE)
            mixed = acc_in[rows, :] * jnp.concatenate([keep, keep], axis=1) + mixed
        if last:
            rest[0][rows, :] = (mixed[:, :HD] / mixed[:, HD:]).astype(rest[0].dtype)
        else:
            rest[0][rows, :] = mixed
            rest[1][rows, :] = new

    scores = scores_of(0)
    for start in range(0, tokens, step):
        following = scores_of(start + step) if start + step < tokens else None
        finish(start, scores)
        scores = following


def attend(flags, queries, tiles, gates, state=None, last=False, part=None, cost=32):
    channels = queries.shape[1]
    tokens = queries.shape[0] if part is None else queries.shape[0] // 2
    heads = channels // HD
    span = tiles[0].shape[1]

    def rows_spec(array, width):
        block = 0 if part is None or array.shape[0] == tokens else part
        return pl.BlockSpec((tokens, width), lambda h: (block, h))

    tile_spec = pl.BlockSpec((2, span, HD), lambda h: (0, 0, h))
    in_specs = [pl.BlockSpec(memory_space=pltpu.SMEM), rows_spec(queries, HD)] + [tile_spec] * len(tiles)
    args = [flags, queries, *tiles]
    if state is not None:
        in_specs += [rows_spec(state[0], 2 * HD), rows_spec(state[1], HD)]
        args += list(state)
    if last:
        out_shape = jax.ShapeDtypeStruct((tokens, channels), jnp.bfloat16)
        out_specs = rows_spec(out_shape, HD)
    else:
        out_shape = [
            jax.ShapeDtypeStruct((tokens, 2 * channels), jnp.float32),
            jax.ShapeDtypeStruct((tokens, channels), jnp.float32),
        ]
        out_specs = [rows_spec(out_shape[0], 2 * HD), rows_spec(out_shape[1], HD)]
    step = 256 if tokens % 256 == 0 else 192
    pairs = len(tiles) * heads * tokens * span
    return pl.pallas_call(
        functools.partial(attend_kernel, tuple(gates), state is None, last, step),
        out_shape=out_shape,
        grid=(heads,),
        in_specs=in_specs,
        out_specs=out_specs,
        compiler_params=pltpu.CompilerParams(vmem_limit_bytes=48 * 1024 * 1024),
        cost_estimate=pl.CostEstimate(flops=pairs * cost, bytes_accessed=1024, transcendentals=0),
    )(*args)


def body(queries, keys_values, out_weight):
    frames, rows, cols, channels = queries.shape
    tokens = frames * rows * cols
    half = channels // 2
    ha_count, wa_count = lax.axis_size("ha"), lax.axis_size("wa")
    ha, wa, ta = lax.axis_index("ha"), lax.axis_index("wa"), lax.axis_index("ta")
    odd = lax.rem(ha, 2)

    q_all = queries.reshape(tokens, channels)
    kv_all = keys_values.reshape(2, tokens, channels)
    keep_at, send_at = odd * half, (1 - odd) * half

    swap_pairs = [(i, i ^ 1) for i in range(ha_count)]
    native_pairs = [(i, (i + (2 if i % 2 else -2)) % ha_count) for i in range(ha_count)]
    swapped_pairs = [(i, (i + (-2 if i % 2 else 2)) % ha_count) for i in range(ha_count)]
    down_pairs = [(i, (i + 1) % wa_count) for i in range(wa_count)]
    up_pairs = [((i + 1) % wa_count, i) for i in range(wa_count)]

    def above_below(cells):
        return lax.ppermute(cells, "wa", down_pairs), lax.ppermute(cells, "wa", up_pairs)

    above, below = wa > 0, wa < wa_count - 1
    low, high = ha >= 2, ha < ha_count - 2
    far_partner = jnp.where(odd == 1, low, high)
    far_native = jnp.where(odd == 1, high, low)
    flags = jnp.stack(
        [above, below, far_partner, far_partner & above, far_partner & below,
         far_native, far_native & above, far_native & below]
    ).astype(jnp.int32)

    kv_send = lax.dynamic_slice_in_dim(kv_all, send_at, half, 2)
    kv_own = lax.dynamic_slice_in_dim(kv_all, keep_at, half, 2)
    q_send = lax.dynamic_slice_in_dim(q_all, send_at, half, 1)
    q_own = lax.dynamic_slice_in_dim(q_all, keep_at, half, 1)

    core, x_hi = lax.rem(ta, 2), ta // 2
    width = out_weight.shape[1] // lax.axis_size("ta")
    ordered = jnp.concatenate(
        [lax.dynamic_slice_in_dim(out_weight, at, half, 0) for at in (keep_at, send_at)], axis=0
    )

    def weight_of(for_core):
        groups = (2 * (1 - x_hi) + for_core, 2 * x_hi + for_core)
        return jnp.concatenate(
            [lax.dynamic_slice_in_dim(ordered, group * width, width, 1) for group in groups], axis=1
        )

    weight_send, weight_keep = weight_of(1 - core), weight_of(core)

    kv_pair = lax.ppermute(kv_send, "ha", swap_pairs)
    own_up, own_down = above_below(kv_own)
    far_p = lax.ppermute(kv_own, "ha", native_pairs)
    flags, weight_send, weight_keep = lax.optimization_barrier((flags, weight_send, weight_keep))
    state_n = attend(flags, q_own, [kv_own], [None])
    kv_pair, q_send, state_n = lax.optimization_barrier((kv_pair, q_send, state_n))
    q_pair = lax.ppermute(q_send, "ha", swap_pairs)
    pair_up, pair_down = above_below(kv_pair)
    far_n = lax.ppermute(kv_pair, "ha", swapped_pairs)
    far_p_up = lax.ppermute(own_up, "ha", native_pairs)
    far_p_down = lax.ppermute(own_down, "ha", native_pairs)
    state_n = attend(flags, q_own, [kv_pair, own_up, own_down], [None, 0, 1], state_n, cost=COST2)
    q_pair, state_n = lax.optimization_barrier((q_pair, state_n))
    state_p = attend(flags, q_pair, [kv_own, kv_pair, own_up, own_down, far_p], [None, None, 0, 1, 2])
    far_n, state_p = lax.optimization_barrier((far_n, state_p))
    far_n_up, far_n_down = above_below(far_n)
    state_p = attend(flags, q_pair, [pair_up, pair_down], [0, 1], state_p)
    state_n, state_p = lax.optimization_barrier((state_n, state_p))
    first_n = attend(flags, q_own, [pair_up, pair_down, far_n], [0, 1, 5], state_n, part=0)
    state_p, first_n, state_n = lax.optimization_barrier((state_p, first_n, state_n))
    backs = []
    for part in (0, 1):
        out_p = attend(flags, q_pair, [far_p_up, far_p_down], [3, 4], state_p, last=True, part=part)
        if part == 0:
            state_p, out_p = lax.optimization_barrier((state_p, out_p))
        else:
            first_n, state_n, out_p = lax.optimization_barrier((first_n, state_n, out_p))
        backs.append(lax.ppermute(out_p, "ha", swap_pairs))
    out_0 = attend(flags, q_own, [far_n_up, far_n_down], [6, 7], first_n, last=True, part=0)

    core_pairs = [(i, i ^ 1) for i in range(4)]
    hi_pairs = [(i, i ^ 2) for i in range(4)]

    def project(out_n, back):
        attention = jnp.concatenate([out_n, back], axis=1)
        sent = jnp.dot(attention, weight_send, preferred_element_type=jnp.float32).astype(jnp.bfloat16)
        taken = lax.ppermute(sent, "ta", core_pairs)
        kept = jnp.dot(attention, weight_keep, preferred_element_type=jnp.float32)
        away = (kept[:, :width] + taken[:, :width].astype(jnp.float32)).astype(jnp.bfloat16)
        return away, kept[:, width:] + taken[:, width:].astype(jnp.float32)

    away_0, home_0 = project(out_0, backs[0])
    away_0, state_n = lax.optimization_barrier((away_0, state_n))
    far_0 = lax.ppermute(away_0, "ta", hi_pairs)
    out_1 = attend(
        flags, q_own, [pair_up, pair_down, far_n, far_n_up, far_n_down], [0, 1, 5, 6, 7], state_n,
        last=True, part=1,
    )
    far_0, out_1 = lax.optimization_barrier((far_0, out_1))
    away_1, home_1 = project(out_1, backs[1])
    far_1 = lax.ppermute(away_1, "ta", hi_pairs)
    result = jnp.concatenate(
        [home_0 + far_0.astype(jnp.float32), home_1 + far_1.astype(jnp.float32)], axis=0
    )
    return result.astype(jnp.bfloat16).reshape(frames, rows, cols, width)


def solution(mesh):
    return jax.shard_map(
        body,
        mesh=mesh,
        in_specs=(P(None, "wa", "ha", "ta"), P(None, None, "wa", "ha", "ta"), P("ta", None)),
        out_specs=P(None, "wa", "ha", "ta"),
        check_vma=False,
    )
```

```python
import functools

import jax
import jax.numpy as jnp
from jax import lax
from jax.experimental import pallas as pl
from jax.experimental.pallas import tpu as pltpu
from jax.sharding import PartitionSpec as P

HD = 128
LOG2E = 1.4426950408889634
EXP_SCALE = HD ** (-0.5) * LOG2E
LOW = -1e30
LIMIT = 2.0**60
KEYS = 256


COST2 = 1024


def attend_kernel(gates, first, last, step, *refs):
    flags_ref, q_ref = refs[:2]
    tiles = refs[2 : 2 + len(gates)]
    rest = refs[2 + len(gates) :]
    if not first:
        acc_in, top_in = rest[:2]
        rest = rest[2:]
    tokens = q_ref.shape[0]
    span = tiles[0].shape[1]
    inside = [None if gate is None else flags_ref[gate] > 0 for gate in gates]
    ones = jnp.ones((span, HD), jnp.bfloat16)

    def scores_of(queries, tile, begin, size):
        return lax.dot_general(
            queries, tile[0, pl.ds(begin, size), :], (((1,), (1,)), ((), ())),
            preferred_element_type=jnp.float32,
        )

    def row_max(scores):
        return jnp.broadcast_to(jnp.max(scores, axis=1, keepdims=True), (scores.shape[0], HD))

    def weights_of(scores, shift):
        wide = jnp.concatenate([shift] * (scores.shape[1] // HD), axis=1)
        return jnp.exp2((scores - wide) * EXP_SCALE).astype(jnp.bfloat16)

    def store(rows, mixed, top):
        if last:
            rest[0][rows, :] = (mixed[:, :HD] / mixed[:, HD:]).astype(rest[0].dtype)
        else:
            rest[0][rows, :] = mixed
            rest[1][rows, :] = top

    def full_step(start, all_scores):
        rows = pl.ds(start, step)
        old = jnp.full((step, HD), LOW, jnp.float32) if first else top_in[rows, :]
        new = old
        for scores, valid in zip(all_scores, inside):
            largest = row_max(scores)
            new = jnp.maximum(new, largest if valid is None else jnp.where(valid, largest, LOW))
        mixed = None
        for scores, valid, tile in zip(all_scores, inside, tiles):
            weights = weights_of(scores, new if valid is None else jnp.where(valid, new, -LOW))
            values = jnp.concatenate([tile[1], ones], axis=1)
            part = jnp.dot(weights, values, preferred_element_type=jnp.float32)
            mixed = part if mixed is None else mixed + part
        if not first:
            keep = jnp.exp2((old - new) * EXP_SCALE)
            mixed = acc_in[rows, :] * jnp.concatenate([keep, keep], axis=1) + mixed
        store(rows, mixed, new)

    def tile_scores(start):
        queries = q_ref[pl.ds(start, step), :]
        return [scores_of(queries, tile, 0, span) for tile in tiles]

    if first:
        ready = tile_scores(0)
        for start in range(0, tokens, step):
            following = tile_scores(start + step) if start + step < tokens else None
            full_step(start, ready)
            ready = following
        return

    def quick_weights(start):
        rows = pl.ds(start, step)
        queries = q_ref[rows, :]
        top = top_in[rows, :]
        parts = []
        for tile, valid in zip(tiles, inside):
            shift = top if valid is None else jnp.where(valid, top, -LOW)
            for begin in range(0, span, KEYS):
                parts.append(weights_of(scores_of(queries, tile, begin, KEYS), shift))
        return jnp.concatenate(parts, axis=1), top

    values = jnp.concatenate([jnp.concatenate([tile[1], ones], axis=1) for tile in tiles], axis=0)
    totals = None
    ready = quick_weights(0)
    for start in range(0, tokens, step):
        following = quick_weights(start + step) if start + step < tokens else None
        rows = pl.ds(start, step)
        mixed = jnp.dot(ready[0], values, preferred_element_type=jnp.float32)
        total = mixed[:, HD:]
        totals = total if totals is None else jnp.maximum(totals, total)
        store(rows, acc_in[rows, :] + mixed, ready[1])
        ready = following

    @pl.when(jnp.logical_not(jnp.max(totals) < LIMIT))
    def _():
        for start in range(0, tokens, step):
            full_step(start, tile_scores(start))


def attend(flags, queries, tiles, gates, state=None, last=False, part=None, cost=32):
    channels = queries.shape[1]
    tokens = queries.shape[0] if part is None else queries.shape[0] // 2
    heads = channels // HD
    span = queries.shape[0]
    arrays = [tile[0] if isinstance(tile, tuple) else tile for tile in tiles]

    def tile_spec(tile):
        if isinstance(tile, tuple):
            return pl.BlockSpec((None, 2, span, HD), lambda h: (tile[1], 0, 0, h))
        return pl.BlockSpec((2, span, HD), lambda h: (0, 0, h))

    def rows_spec(array, width):
        block = 0 if part is None or array.shape[0] == tokens else part
        return pl.BlockSpec((tokens, width), lambda h: (block, h))

    in_specs = [pl.BlockSpec(memory_space=pltpu.SMEM), rows_spec(queries, HD)] + [tile_spec(tile) for tile in tiles]
    args = [flags, queries, *arrays]
    if state is not None:
        in_specs += [rows_spec(state[0], 2 * HD), rows_spec(state[1], HD)]
        args += list(state)
    if last:
        out_shape = jax.ShapeDtypeStruct((tokens, channels), jnp.bfloat16)
        out_specs = rows_spec(out_shape, HD)
    else:
        out_shape = [
            jax.ShapeDtypeStruct((tokens, 2 * channels), jnp.float32),
            jax.ShapeDtypeStruct((tokens, channels), jnp.float32),
        ]
        out_specs = [rows_spec(out_shape[0], 2 * HD), rows_spec(out_shape[1], HD)]
    step = 256 if tokens % 256 == 0 else 192
    pairs = len(tiles) * heads * tokens * span
    return pl.pallas_call(
        functools.partial(attend_kernel, tuple(gates), state is None, last, step),
        out_shape=out_shape,
        grid=(heads,),
        in_specs=in_specs,
        out_specs=out_specs,
        compiler_params=pltpu.CompilerParams(vmem_limit_bytes=48 * 1024 * 1024),
        cost_estimate=pl.CostEstimate(flops=pairs * cost, bytes_accessed=1024, transcendentals=0),
    )(*args)


def body(queries, keys_values, out_weight):
    frames, rows, cols, channels = queries.shape
    tokens = frames * rows * cols
    half = channels // 2
    ha_count, wa_count = lax.axis_size("ha"), lax.axis_size("wa")
    ha, wa, ta = lax.axis_index("ha"), lax.axis_index("wa"), lax.axis_index("ta")
    odd = lax.rem(ha, 2)

    q_all = queries.reshape(tokens, channels)
    kv_all = keys_values.reshape(2, tokens, channels)
    keep_at, send_at = odd * half, (1 - odd) * half

    swap_pairs = [(i, i ^ 1) for i in range(ha_count)]
    native_pairs = [(i, (i + (2 if i % 2 else -2)) % ha_count) for i in range(ha_count)]
    swapped_pairs = [(i, (i + (-2 if i % 2 else 2)) % ha_count) for i in range(ha_count)]
    down_pairs = [(i, (i + 1) % wa_count) for i in range(wa_count)]
    up_pairs = [((i + 1) % wa_count, i) for i in range(wa_count)]

    def above_below(cells):
        return lax.ppermute(cells, "wa", down_pairs), lax.ppermute(cells, "wa", up_pairs)

    above, below = wa > 0, wa < wa_count - 1
    low, high = ha >= 2, ha < ha_count - 2
    far_partner = jnp.where(odd == 1, low, high)
    far_native = jnp.where(odd == 1, high, low)
    flags = jnp.stack(
        [above, below, far_partner, far_partner & above, far_partner & below,
         far_native, far_native & above, far_native & below]
    ).astype(jnp.int32)

    kv_send = lax.dynamic_slice_in_dim(kv_all, send_at, half, 2)
    kv_own = lax.dynamic_slice_in_dim(kv_all, keep_at, half, 2)
    q_send = lax.dynamic_slice_in_dim(q_all, send_at, half, 1)
    q_own = lax.dynamic_slice_in_dim(q_all, keep_at, half, 1)

    kv_pair = lax.ppermute(kv_send, "ha", swap_pairs)

    core, x_hi = lax.rem(ta, 2), ta // 2
    width = out_weight.shape[1] // lax.axis_size("ta")
    ordered = jnp.concatenate(
        [lax.dynamic_slice_in_dim(out_weight, at, half, 0) for at in (keep_at, send_at)], axis=0
    )

    def weight_of(for_core):
        groups = (2 * (1 - x_hi) + for_core, 2 * x_hi + for_core)
        return jnp.concatenate(
            [lax.dynamic_slice_in_dim(ordered, group * width, width, 1) for group in groups], axis=1
        )

    weight_send, weight_keep = weight_of(1 - core), weight_of(core)

    own_up, own_down = above_below(kv_own)
    far_p = lax.ppermute(kv_own, "ha", native_pairs)
    flags, weight_send, weight_keep = lax.optimization_barrier((flags, weight_send, weight_keep))
    state_n = attend(flags, q_own, [kv_own], [None])
    kv_pair, q_send, state_n, own_up, own_down, far_p = lax.optimization_barrier(
        (kv_pair, q_send, state_n, own_up, own_down, far_p)
    )
    q_pair = lax.ppermute(q_send, "ha", swap_pairs)
    pair_up, pair_down = above_below(kv_pair)
    far_n = lax.ppermute(kv_pair, "ha", swapped_pairs)
    far_p_rows = lax.ppermute(jnp.stack([own_up, own_down]), "ha", native_pairs)
    state_n = attend(flags, q_own, [kv_pair, own_up, own_down], [None, 0, 1], state_n, cost=COST2)
    q_pair, state_n = lax.optimization_barrier((q_pair, state_n))
    state_p = attend(flags, q_pair, [kv_own, kv_pair, own_up, own_down, far_p], [None, None, 0, 1, 2])
    far_n, state_p = lax.optimization_barrier((far_n, state_p))
    far_n_up, far_n_down = above_below(far_n)
    state_p = attend(flags, q_pair, [pair_up, pair_down], [0, 1], state_p)
    state_n, state_p = lax.optimization_barrier((state_n, state_p))
    first_n = attend(flags, q_own, [pair_up, pair_down, far_n], [0, 1, 5], state_n, part=0)
    state_p, first_n, state_n = lax.optimization_barrier((state_p, first_n, state_n))
    backs = []
    for part in (0, 1):
        out_p = attend(flags, q_pair, [(far_p_rows, 0), (far_p_rows, 1)], [3, 4], state_p, last=True, part=part)
        if part == 0:
            state_p, out_p = lax.optimization_barrier((state_p, out_p))
        else:
            first_n, state_n, out_p = lax.optimization_barrier((first_n, state_n, out_p))
        backs.append(lax.ppermute(out_p, "ha", swap_pairs))
    out_0 = attend(flags, q_own, [far_n_up, far_n_down], [6, 7], first_n, last=True, part=0)

    core_pairs = [(i, i ^ 1) for i in range(4)]
    hi_pairs = [(i, i ^ 2) for i in range(4)]

    def project(out_n, back, earlier=None):
        attention = jnp.concatenate([out_n, back], axis=1)
        sent = jnp.dot(attention, weight_send, preferred_element_type=jnp.float32).astype(jnp.bfloat16)
        if earlier is not None:
            sent, _ = lax.optimization_barrier((sent, earlier))
        taken = lax.ppermute(sent, "ta", core_pairs)
        kept = jnp.dot(attention, weight_keep, preferred_element_type=jnp.float32)
        away = (kept[:, :width] + taken[:, :width].astype(jnp.float32)).astype(jnp.bfloat16)
        return away, kept[:, width:] + taken[:, width:].astype(jnp.float32)

    away_0, home_0 = project(out_0, backs[0])
    away_0, back_1, state_n = lax.optimization_barrier((away_0, backs[1], state_n))
    far_0 = lax.ppermute(away_0, "ta", hi_pairs)
    out_1 = attend(
        flags, q_own, [pair_up, pair_down, far_n, far_n_up, far_n_down], [0, 1, 5, 6, 7], state_n,
        last=True, part=1,
    )
    away_1, home_1 = project(out_1, back_1, far_0)
    far_1 = lax.ppermute(away_1, "ta", hi_pairs)
    result = jnp.concatenate(
        [home_0 + far_0.astype(jnp.float32), home_1 + far_1.astype(jnp.float32)], axis=0
    )
    return result.astype(jnp.bfloat16).reshape(frames, rows, cols, width)


def solution(mesh):
    return jax.shard_map(
        body,
        mesh=mesh,
        in_specs=(P(None, "wa", "ha", "ta"), P(None, None, "wa", "ha", "ta"), P("ta", None)),
        out_specs=P(None, "wa", "ha", "ta"),
        check_vma=False,
    )
```

```python
import functools

import jax
import jax.numpy as jnp
from jax import lax
from jax.experimental import pallas as pl
from jax.experimental.pallas import tpu as pltpu
from jax.sharding import PartitionSpec as P

HD = 128
LOG2E = 1.4426950408889634
EXP_SCALE = HD ** (-0.5) * LOG2E
LOW = -1e30
LIMIT = 2.0**60
KEYS = 256


COST2 = 1024


def attend_kernel(gates, first, last, step, *refs):
    flags_ref, q_ref = refs[:2]
    tiles = refs[2 : 2 + len(gates)]
    rest = refs[2 + len(gates) :]
    if not first:
        acc_in, top_in = rest[:2]
        rest = rest[2:]
    tokens = q_ref.shape[0]
    span = tiles[0].shape[1]
    inside = [None if gate is None else flags_ref[gate] > 0 for gate in gates]
    ones = jnp.ones((span, HD), jnp.bfloat16)

    def scores_of(queries, tile, begin, size):
        return lax.dot_general(
            queries, tile[0, pl.ds(begin, size), :], (((1,), (1,)), ((), ())),
            preferred_element_type=jnp.float32,
        )

    def row_max(scores):
        return jnp.broadcast_to(jnp.max(scores, axis=1, keepdims=True), (scores.shape[0], HD))

    def weights_of(scores, shift):
        wide = jnp.concatenate([shift] * (scores.shape[1] // HD), axis=1)
        return jnp.exp2((scores - wide) * EXP_SCALE).astype(jnp.bfloat16)

    def store(rows, mixed, top):
        if last:
            rest[0][rows, :] = (mixed[:, :HD] / mixed[:, HD:]).astype(rest[0].dtype)
        else:
            rest[0][rows, :] = mixed
            rest[1][rows, :] = top

    def full_step(start, all_scores):
        rows = pl.ds(start, step)
        old = jnp.full((step, HD), LOW, jnp.float32) if first else top_in[rows, :]
        new = old
        for scores, valid in zip(all_scores, inside):
            largest = row_max(scores)
            new = jnp.maximum(new, largest if valid is None else jnp.where(valid, largest, LOW))
        mixed = None
        for scores, valid, tile in zip(all_scores, inside, tiles):
            weights = weights_of(scores, new if valid is None else jnp.where(valid, new, -LOW))
            values = jnp.concatenate([tile[1], ones], axis=1)
            part = jnp.dot(weights, values, preferred_element_type=jnp.float32)
            mixed = part if mixed is None else mixed + part
        if not first:
            keep = jnp.exp2((old - new) * EXP_SCALE)
            mixed = acc_in[rows, :] * jnp.concatenate([keep, keep], axis=1) + mixed
        store(rows, mixed, new)

    def tile_scores(start):
        queries = q_ref[pl.ds(start, step), :]
        return [scores_of(queries, tile, 0, span) for tile in tiles]

    if first:
        ready = tile_scores(0)
        for start in range(0, tokens, step):
            following = tile_scores(start + step) if start + step < tokens else None
            full_step(start, ready)
            ready = following
        return

    def quick_weights(start):
        rows = pl.ds(start, step)
        queries = q_ref[rows, :]
        top = top_in[rows, :]
        parts = []
        for tile, valid in zip(tiles, inside):
            shift = top if valid is None else jnp.where(valid, top, -LOW)
            for begin in range(0, span, KEYS):
                parts.append(weights_of(scores_of(queries, tile, begin, KEYS), shift))
        return jnp.concatenate(parts, axis=1), top

    values = jnp.concatenate([jnp.concatenate([tile[1], ones], axis=1) for tile in tiles], axis=0)
    totals = None
    ready = quick_weights(0)
    for start in range(0, tokens, step):
        following = quick_weights(start + step) if start + step < tokens else None
        rows = pl.ds(start, step)
        mixed = jnp.dot(ready[0], values, preferred_element_type=jnp.float32)
        total = mixed[:, HD:]
        totals = total if totals is None else jnp.maximum(totals, total)
        store(rows, acc_in[rows, :] + mixed, ready[1])
        ready = following

    @pl.when(jnp.logical_not(jnp.max(totals) < LIMIT))
    def _():
        for start in range(0, tokens, step):
            full_step(start, tile_scores(start))


def attend(flags, queries, tiles, gates, state=None, last=False, part=None, cost=32):
    channels = queries.shape[1]
    tokens = queries.shape[0] if part is None else queries.shape[0] // 2
    heads = channels // HD
    span = queries.shape[0]
    arrays = [tile[0] if isinstance(tile, tuple) else tile for tile in tiles]

    def tile_spec(tile):
        if isinstance(tile, tuple):
            return pl.BlockSpec((None, 2, span, HD), lambda h: (tile[1], 0, 0, h))
        return pl.BlockSpec((2, span, HD), lambda h: (0, 0, h))

    def rows_spec(array, width):
        block = 0 if part is None or array.shape[0] == tokens else part
        return pl.BlockSpec((tokens, width), lambda h: (block, h))

    in_specs = [pl.BlockSpec(memory_space=pltpu.SMEM), rows_spec(queries, HD)] + [tile_spec(tile) for tile in tiles]
    args = [flags, queries, *arrays]
    if state is not None:
        in_specs += [rows_spec(state[0], 2 * HD), rows_spec(state[1], HD)]
        args += list(state)
    if last:
        out_shape = jax.ShapeDtypeStruct((tokens, channels), jnp.bfloat16)
        out_specs = rows_spec(out_shape, HD)
    else:
        out_shape = [
            jax.ShapeDtypeStruct((tokens, 2 * channels), jnp.float32),
            jax.ShapeDtypeStruct((tokens, channels), jnp.float32),
        ]
        out_specs = [rows_spec(out_shape[0], 2 * HD), rows_spec(out_shape[1], HD)]
    step = 256 if tokens % 256 == 0 else 192
    pairs = len(tiles) * heads * tokens * span
    return pl.pallas_call(
        functools.partial(attend_kernel, tuple(gates), state is None, last, step),
        out_shape=out_shape,
        grid=(heads,),
        in_specs=in_specs,
        out_specs=out_specs,
        compiler_params=pltpu.CompilerParams(vmem_limit_bytes=48 * 1024 * 1024),
        cost_estimate=pl.CostEstimate(flops=pairs * cost, bytes_accessed=1024, transcendentals=0),
    )(*args)


def body(queries, keys_values, out_weight):
    frames, rows, cols, channels = queries.shape
    tokens = frames * rows * cols
    half = channels // 2
    ha_count, wa_count = lax.axis_size("ha"), lax.axis_size("wa")
    ha, wa, ta = lax.axis_index("ha"), lax.axis_index("wa"), lax.axis_index("ta")
    odd = lax.rem(ha, 2)

    q_all = queries.reshape(tokens, channels)
    kv_all = keys_values.reshape(2, tokens, channels)
    keep_at, send_at = odd * half, (1 - odd) * half

    swap_pairs = [(i, i ^ 1) for i in range(ha_count)]
    native_pairs = [(i, (i + (2 if i % 2 else -2)) % ha_count) for i in range(ha_count)]
    swapped_pairs = [(i, (i + (-2 if i % 2 else 2)) % ha_count) for i in range(ha_count)]
    down_pairs = [(i, (i + 1) % wa_count) for i in range(wa_count)]
    up_pairs = [((i + 1) % wa_count, i) for i in range(wa_count)]

    def above_below(cells):
        return lax.ppermute(cells, "wa", down_pairs), lax.ppermute(cells, "wa", up_pairs)

    above, below = wa > 0, wa < wa_count - 1
    low, high = ha >= 2, ha < ha_count - 2
    far_partner = jnp.where(odd == 1, low, high)
    far_native = jnp.where(odd == 1, high, low)
    flags = jnp.stack(
        [above, below, far_partner, far_partner & above, far_partner & below,
         far_native, far_native & above, far_native & below]
    ).astype(jnp.int32)

    kv_send = lax.dynamic_slice_in_dim(kv_all, send_at, half, 2)
    kv_send, kv_all = lax.optimization_barrier((kv_send, kv_all))
    kv_own = lax.dynamic_slice_in_dim(kv_all, keep_at, half, 2)
    q_send = lax.dynamic_slice_in_dim(q_all, send_at, half, 1)
    q_own = lax.dynamic_slice_in_dim(q_all, keep_at, half, 1)

    core, x_hi = lax.rem(ta, 2), ta // 2
    width = out_weight.shape[1] // lax.axis_size("ta")
    ordered = jnp.concatenate(
        [lax.dynamic_slice_in_dim(out_weight, at, half, 0) for at in (keep_at, send_at)], axis=0
    )
    groups = (2 * (1 - x_hi) + 1 - core, 2 * (1 - x_hi) + core, 2 * x_hi + 1 - core, ta)
    weights = [lax.dynamic_slice_in_dim(ordered, group * width, width, 1) for group in groups]

    kv_pair = lax.ppermute(kv_send, "ha", swap_pairs)
    own_up, own_down = above_below(kv_own)
    far_p = lax.ppermute(kv_own, "ha", native_pairs)
    flags, *weights = lax.optimization_barrier((flags, *weights))
    state_n = attend(flags, q_own, [kv_own], [None])
    own_up, own_down, state_n = lax.optimization_barrier((own_up, own_down, state_n))
    far_p_rows = lax.ppermute(jnp.stack([own_up, own_down]), "ha", native_pairs)
    kv_pair, q_send, state_n, far_p = lax.optimization_barrier((kv_pair, q_send, state_n, far_p))
    q_pair = lax.ppermute(q_send, "ha", swap_pairs)
    pair_up, pair_down = above_below(kv_pair)
    far_n = lax.ppermute(kv_pair, "ha", swapped_pairs)

    state_n = attend(flags, q_own, [kv_pair, own_up, own_down], [None, 0, 1], state_n)
    q_pair, state_n = lax.optimization_barrier((q_pair, state_n))
    state_p = attend(flags, q_pair, [kv_own, kv_pair, own_up, own_down, far_p], [None, None, 0, 1, 2])
    far_n, state_p = lax.optimization_barrier((far_n, state_p))
    far_n_up, far_n_down = above_below(far_n)
    state_p = attend(flags, q_pair, [pair_up, pair_down], [0, 1], state_p)
    state_n, state_p = lax.optimization_barrier((state_n, state_p))
    state_n = attend(flags, q_own, [pair_up, pair_down, far_n], [0, 1, 5], state_n)
    state_p, state_n = lax.optimization_barrier((state_p, state_n))
    out_p = attend(flags, q_pair, [(far_p_rows, 0), (far_p_rows, 1)], [3, 4], state_p, last=True)
    state_n, out_p = lax.optimization_barrier((state_n, out_p))
    back = lax.ppermute(out_p, "ha", swap_pairs)
    out_n = attend(flags, q_own, [far_n_up, far_n_down], [6, 7], state_n, last=True)

    core_pairs = [(i, i ^ 1) for i in range(4)]
    hi_pairs = [(i, i ^ 2) for i in range(4)]
    attention = jnp.concatenate([out_n, back], axis=1)

    def partial_of(weight):
        return jnp.dot(attention, weight, preferred_element_type=jnp.float32)

    away_sent = partial_of(weights[0]).astype(jnp.bfloat16)
    away_taken = lax.ppermute(away_sent, "ta", core_pairs)
    away = (partial_of(weights[1]) + away_taken.astype(jnp.float32)).astype(jnp.bfloat16)
    far = lax.ppermute(away, "ta", hi_pairs)
    home_sent = partial_of(weights[2]).astype(jnp.bfloat16)
    home_taken = lax.ppermute(home_sent, "ta", core_pairs)
    home = partial_of(weights[3]) + home_taken.astype(jnp.float32)
    result = home + far.astype(jnp.float32)
    return result.astype(jnp.bfloat16).reshape(frames, rows, cols, width)


def solution(mesh):
    return jax.shard_map(
        body,
        mesh=mesh,
        in_specs=(P(None, "wa", "ha", "ta"), P(None, None, "wa", "ha", "ta"), P("ta", None)),
        out_specs=P(None, "wa", "ha", "ta"),
        check_vma=False,
    )
```

```python
import functools

import jax
import jax.numpy as jnp
from jax import lax
from jax.experimental import pallas as pl
from jax.experimental.pallas import tpu as pltpu
from jax.sharding import PartitionSpec as P

HD = 128
LOG2E = 1.4426950408889634
EXP_SCALE = HD ** (-0.5) * LOG2E
LOW = -1e30
LIMIT = 2.0**60
KEYS = 256


COST2 = 1024


def attend_kernel(gates, first, last, step, *refs):
    flags_ref, q_ref = refs[:2]
    tiles = refs[2 : 2 + len(gates)]
    rest = refs[2 + len(gates) :]
    if not first:
        acc_in, top_in = rest[:2]
        rest = rest[2:]
    tokens = q_ref.shape[0]
    span = tiles[0].shape[1]
    inside = [None if gate is None else flags_ref[gate] > 0 for gate in gates]
    ones = jnp.ones((span, HD), jnp.bfloat16)

    def scores_of(queries, tile, begin, size):
        return lax.dot_general(
            queries, tile[0, pl.ds(begin, size), :], (((1,), (1,)), ((), ())),
            preferred_element_type=jnp.float32,
        )

    def row_max(scores):
        return jnp.broadcast_to(jnp.max(scores, axis=1, keepdims=True), (scores.shape[0], HD))

    def weights_of(scores, shift):
        wide = jnp.concatenate([shift] * (scores.shape[1] // HD), axis=1)
        return jnp.exp2((scores - wide) * EXP_SCALE).astype(jnp.bfloat16)

    def store(rows, mixed, top):
        if last:
            rest[0][rows, :] = (mixed[:, :HD] / mixed[:, HD:]).astype(rest[0].dtype)
        else:
            rest[0][rows, :] = mixed
            rest[1][rows, :] = top

    def full_step(start, all_scores):
        rows = pl.ds(start, step)
        old = jnp.full((step, HD), LOW, jnp.float32) if first else top_in[rows, :]
        new = old
        for scores, valid in zip(all_scores, inside):
            largest = row_max(scores)
            new = jnp.maximum(new, largest if valid is None else jnp.where(valid, largest, LOW))
        mixed = None
        for scores, valid, tile in zip(all_scores, inside, tiles):
            weights = weights_of(scores, new if valid is None else jnp.where(valid, new, -LOW))
            values = jnp.concatenate([tile[1], ones], axis=1)
            part = jnp.dot(weights, values, preferred_element_type=jnp.float32)
            mixed = part if mixed is None else mixed + part
        if not first:
            keep = jnp.exp2((old - new) * EXP_SCALE)
            mixed = acc_in[rows, :] * jnp.concatenate([keep, keep], axis=1) + mixed
        store(rows, mixed, new)

    def tile_scores(start):
        queries = q_ref[pl.ds(start, step), :]
        return [scores_of(queries, tile, 0, span) for tile in tiles]

    if first:
        ready = tile_scores(0)
        for start in range(0, tokens, step):
            following = tile_scores(start + step) if start + step < tokens else None
            full_step(start, ready)
            ready = following
        return

    def quick_weights(start):
        rows = pl.ds(start, step)
        queries = q_ref[rows, :]
        top = top_in[rows, :]
        parts = []
        for tile, valid in zip(tiles, inside):
            shift = top if valid is None else jnp.where(valid, top, -LOW)
            for begin in range(0, span, KEYS):
                parts.append(weights_of(scores_of(queries, tile, begin, KEYS), shift))
        return jnp.concatenate(parts, axis=1), top

    values = jnp.concatenate([jnp.concatenate([tile[1], ones], axis=1) for tile in tiles], axis=0)
    totals = None
    ready = quick_weights(0)
    for start in range(0, tokens, step):
        following = quick_weights(start + step) if start + step < tokens else None
        rows = pl.ds(start, step)
        mixed = jnp.dot(ready[0], values, preferred_element_type=jnp.float32)
        total = mixed[:, HD:]
        totals = total if totals is None else jnp.maximum(totals, total)
        store(rows, acc_in[rows, :] + mixed, ready[1])
        ready = following

    @pl.when(jnp.logical_not(jnp.max(totals) < LIMIT))
    def _():
        for start in range(0, tokens, step):
            full_step(start, tile_scores(start))


def attend(flags, queries, tiles, gates, state=None, last=False, part=None, cost=32):
    channels = queries.shape[1]
    tokens = queries.shape[0] if part is None else queries.shape[0] // 2
    heads = channels // HD
    span = queries.shape[0]
    arrays = [tile[0] if isinstance(tile, tuple) else tile for tile in tiles]

    def tile_spec(tile):
        if isinstance(tile, tuple):
            return pl.BlockSpec((None, 2, span, HD), lambda h: (tile[1], 0, 0, h))
        return pl.BlockSpec((2, span, HD), lambda h: (0, 0, h))

    def rows_spec(array, width):
        block = 0 if part is None or array.shape[0] == tokens else part
        return pl.BlockSpec((tokens, width), lambda h: (block, h))

    in_specs = [pl.BlockSpec(memory_space=pltpu.SMEM), rows_spec(queries, HD)] + [tile_spec(tile) for tile in tiles]
    args = [flags, queries, *arrays]
    if state is not None:
        in_specs += [rows_spec(state[0], 2 * HD), rows_spec(state[1], HD)]
        args += list(state)
    if last:
        out_shape = jax.ShapeDtypeStruct((tokens, channels), jnp.bfloat16)
        out_specs = rows_spec(out_shape, HD)
    else:
        out_shape = [
            jax.ShapeDtypeStruct((tokens, 2 * channels), jnp.float32),
            jax.ShapeDtypeStruct((tokens, channels), jnp.float32),
        ]
        out_specs = [rows_spec(out_shape[0], 2 * HD), rows_spec(out_shape[1], HD)]
    step = 256 if tokens % 256 == 0 else 192
    pairs = len(tiles) * heads * tokens * span
    return pl.pallas_call(
        functools.partial(attend_kernel, tuple(gates), state is None, last, step),
        out_shape=out_shape,
        grid=(heads,),
        in_specs=in_specs,
        out_specs=out_specs,
        compiler_params=pltpu.CompilerParams(vmem_limit_bytes=48 * 1024 * 1024),
        cost_estimate=pl.CostEstimate(flops=pairs * cost, bytes_accessed=1024, transcendentals=0),
    )(*args)


def pass_flags(flags):
    def copy_kernel(in_ref, out_ref):
        for index in range(flags.shape[0]):
            out_ref[index] = in_ref[index]

    spec = pl.BlockSpec(memory_space=pltpu.SMEM)
    return pl.pallas_call(
        copy_kernel,
        out_shape=jax.ShapeDtypeStruct(flags.shape, flags.dtype),
        in_specs=[spec],
        out_specs=spec,
        cost_estimate=pl.CostEstimate(flops=4 * 10**9, bytes_accessed=64, transcendentals=0),
    )(flags)


def body(queries, keys_values, out_weight):
    frames, rows, cols, channels = queries.shape
    tokens = frames * rows * cols
    half = channels // 2
    ha_count, wa_count = lax.axis_size("ha"), lax.axis_size("wa")
    ha, wa, ta = lax.axis_index("ha"), lax.axis_index("wa"), lax.axis_index("ta")
    odd = lax.rem(ha, 2)

    q_all = queries.reshape(tokens, channels)
    kv_all = keys_values.reshape(2, tokens, channels)
    keep_at, send_at = odd * half, (1 - odd) * half

    swap_pairs = [(i, i ^ 1) for i in range(ha_count)]
    native_pairs = [(i, (i + (2 if i % 2 else -2)) % ha_count) for i in range(ha_count)]
    swapped_pairs = [(i, (i + (-2 if i % 2 else 2)) % ha_count) for i in range(ha_count)]
    down_pairs = [(i, (i + 1) % wa_count) for i in range(wa_count)]
    up_pairs = [((i + 1) % wa_count, i) for i in range(wa_count)]

    def above_below(cells):
        return lax.ppermute(cells, "wa", down_pairs), lax.ppermute(cells, "wa", up_pairs)

    above, below = wa > 0, wa < wa_count - 1
    low, high = ha >= 2, ha < ha_count - 2
    far_partner = jnp.where(odd == 1, low, high)
    far_native = jnp.where(odd == 1, high, low)
    flags = jnp.stack(
        [above, below, far_partner, far_partner & above, far_partner & below,
         far_native, far_native & above, far_native & below]
    ).astype(jnp.int32)

    kv_send = lax.dynamic_slice_in_dim(kv_all, send_at, half, 2)
    kv_send, kv_all = lax.optimization_barrier((kv_send, kv_all))
    kv_own = lax.dynamic_slice_in_dim(kv_all, keep_at, half, 2)
    q_send = lax.dynamic_slice_in_dim(q_all, send_at, half, 1)
    q_own = lax.dynamic_slice_in_dim(q_all, keep_at, half, 1)

    core, x_hi = lax.rem(ta, 2), ta // 2
    width = out_weight.shape[1] // lax.axis_size("ta")
    ordered = jnp.concatenate(
        [lax.dynamic_slice_in_dim(out_weight, at, half, 0) for at in (keep_at, send_at)], axis=0
    )
    groups = (2 * (1 - x_hi) + 1 - core, 2 * (1 - x_hi) + core, 2 * x_hi + 1 - core, ta)
    weights = [lax.dynamic_slice_in_dim(ordered, group * width, width, 1) for group in groups]

    kv_pair = lax.ppermute(kv_send, "ha", swap_pairs)
    own_up, own_down = above_below(kv_own)
    far_p = lax.ppermute(kv_own, "ha", native_pairs)
    flags, *weights = lax.optimization_barrier((flags, *weights))
    state_n = attend(flags, q_own, [kv_own], [None])
    kv_pair, q_send, state_n, flags = lax.optimization_barrier((kv_pair, q_send, state_n, flags))
    q_pair = lax.ppermute(q_send, "ha", swap_pairs)
    pair_up, pair_down = above_below(kv_pair)
    far_n = lax.ppermute(kv_pair, "ha", swapped_pairs)
    flags = pass_flags(flags)
    own_up, own_down, far_p, flags = lax.optimization_barrier((own_up, own_down, far_p, flags))
    far_p_rows = lax.ppermute(jnp.stack([own_up, own_down]), "ha", native_pairs)

    state_n = attend(flags, q_own, [kv_pair, own_up, own_down], [None, 0, 1], state_n)
    q_pair, state_n = lax.optimization_barrier((q_pair, state_n))
    state_p = attend(flags, q_pair, [kv_own, kv_pair, own_up, own_down, far_p], [None, None, 0, 1, 2])
    far_n, state_p = lax.optimization_barrier((far_n, state_p))
    far_n_up, far_n_down = above_below(far_n)
    state_p = attend(flags, q_pair, [pair_up, pair_down], [0, 1], state_p)
    state_n, state_p = lax.optimization_barrier((state_n, state_p))
    state_n = attend(flags, q_own, [pair_up, pair_down, far_n], [0, 1, 5], state_n)
    state_p, state_n = lax.optimization_barrier((state_p, state_n))
    out_p = attend(flags, q_pair, [(far_p_rows, 0), (far_p_rows, 1)], [3, 4], state_p, last=True)
    state_n, out_p = lax.optimization_barrier((state_n, out_p))
    back = lax.ppermute(out_p, "ha", swap_pairs)
    out_n = attend(flags, q_own, [far_n_up, far_n_down], [6, 7], state_n, last=True)

    core_pairs = [(i, i ^ 1) for i in range(4)]
    hi_pairs = [(i, i ^ 2) for i in range(4)]
    attention = jnp.concatenate([out_n, back], axis=1)

    def partial_of(group):
        return jnp.dot(attention, weights[group], preferred_element_type=jnp.float32)

    away_sent = partial_of(0).astype(jnp.bfloat16)
    away_taken = lax.ppermute(away_sent, "ta", core_pairs)
    away = (partial_of(1) + away_taken.astype(jnp.float32)).astype(jnp.bfloat16)
    far = lax.ppermute(away, "ta", hi_pairs)
    home_sent = partial_of(2).astype(jnp.bfloat16)
    home_taken = lax.ppermute(home_sent, "ta", core_pairs)
    home = partial_of(3) + home_taken.astype(jnp.float32)
    result = home + far.astype(jnp.float32)
    return result.astype(jnp.bfloat16).reshape(frames, rows, cols, width)


def solution(mesh):
    return jax.shard_map(
        body,
        mesh=mesh,
        in_specs=(P(None, "wa", "ha", "ta"), P(None, None, "wa", "ha", "ta"), P("ta", None)),
        out_specs=P(None, "wa", "ha", "ta"),
        check_vma=False,
    )
```

```python
import functools

import jax
import jax.numpy as jnp
from jax import lax
from jax.experimental import pallas as pl
from jax.experimental.pallas import tpu as pltpu
from jax.sharding import PartitionSpec as P

HD = 128
LOG2E = 1.4426950408889634
EXP_SCALE = HD ** (-0.5) * LOG2E
LOW = -1e30
LIMIT = 2.0**60
KEYS = 256


COST2 = 1024
COST3 = 32


def attend_kernel(gates, first, last, step, *refs):
    flags_ref, q_ref = refs[:2]
    tiles = refs[2 : 2 + len(gates)]
    rest = refs[2 + len(gates) :]
    if not first:
        acc_in, top_in = rest[:2]
        rest = rest[2:]
    tokens = q_ref.shape[0]
    span = tiles[0].shape[1]
    inside = [None if gate is None else flags_ref[gate] > 0 for gate in gates]
    ones = jnp.ones((span, HD), jnp.bfloat16)

    def scores_of(queries, tile, begin, size):
        return lax.dot_general(
            queries, tile[0, pl.ds(begin, size), :], (((1,), (1,)), ((), ())),
            preferred_element_type=jnp.float32,
        )

    def row_max(scores):
        return jnp.broadcast_to(jnp.max(scores, axis=1, keepdims=True), (scores.shape[0], HD))

    def weights_of(scores, shift):
        wide = jnp.concatenate([shift] * (scores.shape[1] // HD), axis=1)
        return jnp.exp2((scores - wide) * EXP_SCALE).astype(jnp.bfloat16)

    def store(rows, mixed, top):
        if last:
            rest[0][rows, :] = (mixed[:, :HD] / mixed[:, HD:]).astype(rest[0].dtype)
        else:
            rest[0][rows, :] = mixed
            rest[1][rows, :] = top

    def full_step(start, all_scores):
        rows = pl.ds(start, step)
        old = jnp.full((step, HD), LOW, jnp.float32) if first else top_in[rows, :]
        new = old
        for scores, valid in zip(all_scores, inside):
            largest = row_max(scores)
            new = jnp.maximum(new, largest if valid is None else jnp.where(valid, largest, LOW))
        mixed = None
        for scores, valid, tile in zip(all_scores, inside, tiles):
            weights = weights_of(scores, new if valid is None else jnp.where(valid, new, -LOW))
            values = jnp.concatenate([tile[1], ones], axis=1)
            part = jnp.dot(weights, values, preferred_element_type=jnp.float32)
            mixed = part if mixed is None else mixed + part
        if not first:
            keep = jnp.exp2((old - new) * EXP_SCALE)
            mixed = acc_in[rows, :] * jnp.concatenate([keep, keep], axis=1) + mixed
        store(rows, mixed, new)

    def tile_scores(start):
        queries = q_ref[pl.ds(start, step), :]
        return [scores_of(queries, tile, 0, span) for tile in tiles]

    if first:
        ready = tile_scores(0)
        for start in range(0, tokens, step):
            following = tile_scores(start + step) if start + step < tokens else None
            full_step(start, ready)
            ready = following
        return

    def quick_weights(start):
        rows = pl.ds(start, step)
        queries = q_ref[rows, :]
        top = top_in[rows, :]
        parts = []
        for tile, valid in zip(tiles, inside):
            shift = top if valid is None else jnp.where(valid, top, -LOW)
            for begin in range(0, span, KEYS):
                parts.append(weights_of(scores_of(queries, tile, begin, KEYS), shift))
        return jnp.concatenate(parts, axis=1), top

    values = jnp.concatenate([jnp.concatenate([tile[1], ones], axis=1) for tile in tiles], axis=0)
    totals = None
    ready = quick_weights(0)
    for start in range(0, tokens, step):
        following = quick_weights(start + step) if start + step < tokens else None
        rows = pl.ds(start, step)
        mixed = jnp.dot(ready[0], values, preferred_element_type=jnp.float32)
        total = mixed[:, HD:]
        totals = total if totals is None else jnp.maximum(totals, total)
        store(rows, acc_in[rows, :] + mixed, ready[1])
        ready = following

    @pl.when(jnp.logical_not(jnp.max(totals) < LIMIT))
    def _():
        for start in range(0, tokens, step):
            full_step(start, tile_scores(start))


def attend(flags, queries, tiles, gates, state=None, last=False, part=None, cost=32):
    channels = queries.shape[1]
    tokens = queries.shape[0] if part is None else queries.shape[0] // 2
    heads = channels // HD
    span = queries.shape[0]
    arrays = [tile[0] if isinstance(tile, tuple) else tile for tile in tiles]

    def tile_spec(tile):
        if isinstance(tile, tuple):
            return pl.BlockSpec((None, 2, span, HD), lambda h: (tile[1], 0, 0, h))
        return pl.BlockSpec((2, span, HD), lambda h: (0, 0, h))

    def rows_spec(array, width):
        block = 0 if part is None or array.shape[0] == tokens else part
        return pl.BlockSpec((tokens, width), lambda h: (block, h))

    in_specs = [pl.BlockSpec(memory_space=pltpu.SMEM), rows_spec(queries, HD)] + [tile_spec(tile) for tile in tiles]
    args = [flags, queries, *arrays]
    if state is not None:
        in_specs += [rows_spec(state[0], 2 * HD), rows_spec(state[1], HD)]
        args += list(state)
    if last:
        out_shape = jax.ShapeDtypeStruct((tokens, channels), jnp.bfloat16)
        out_specs = rows_spec(out_shape, HD)
    else:
        out_shape = [
            jax.ShapeDtypeStruct((tokens, 2 * channels), jnp.float32),
            jax.ShapeDtypeStruct((tokens, channels), jnp.float32),
        ]
        out_specs = [rows_spec(out_shape[0], 2 * HD), rows_spec(out_shape[1], HD)]
    step = 256 if tokens % 256 == 0 else 192
    pairs = len(tiles) * heads * tokens * span
    return pl.pallas_call(
        functools.partial(attend_kernel, tuple(gates), state is None, last, step),
        out_shape=out_shape,
        grid=(heads,),
        in_specs=in_specs,
        out_specs=out_specs,
        compiler_params=pltpu.CompilerParams(vmem_limit_bytes=28 * 1024 * 1024),
        cost_estimate=pl.CostEstimate(flops=pairs * cost, bytes_accessed=1024, transcendentals=0),
    )(*args)


def body(queries, keys_values, out_weight):
    frames, rows, cols, channels = queries.shape
    tokens = frames * rows * cols
    half = channels // 2
    ha_count, wa_count = lax.axis_size("ha"), lax.axis_size("wa")
    ha, wa, ta = lax.axis_index("ha"), lax.axis_index("wa"), lax.axis_index("ta")
    odd = lax.rem(ha, 2)

    q_all = queries.reshape(tokens, channels)
    kv_all = keys_values.reshape(2, tokens, channels)
    keep_at, send_at = odd * half, (1 - odd) * half

    swap_pairs = [(i, i ^ 1) for i in range(ha_count)]
    native_pairs = [(i, (i + (2 if i % 2 else -2)) % ha_count) for i in range(ha_count)]
    swapped_pairs = [(i, (i + (-2 if i % 2 else 2)) % ha_count) for i in range(ha_count)]
    down_pairs = [(i, (i + 1) % wa_count) for i in range(wa_count)]
    up_pairs = [((i + 1) % wa_count, i) for i in range(wa_count)]

    def above_below(cells):
        return lax.ppermute(cells, "wa", down_pairs), lax.ppermute(cells, "wa", up_pairs)

    above, below = wa > 0, wa < wa_count - 1
    low, high = ha >= 2, ha < ha_count - 2
    far_partner = jnp.where(odd == 1, low, high)
    far_native = jnp.where(odd == 1, high, low)
    flags = jnp.stack(
        [above, below, far_partner, far_partner & above, far_partner & below,
         far_native, far_native & above, far_native & below]
    ).astype(jnp.int32)

    kv_send = lax.dynamic_slice_in_dim(kv_all, send_at, half, 2)
    kv_send, kv_all = lax.optimization_barrier((kv_send, kv_all))
    kv_own = lax.dynamic_slice_in_dim(kv_all, keep_at, half, 2)
    q_send = lax.dynamic_slice_in_dim(q_all, send_at, half, 1)
    q_own = lax.dynamic_slice_in_dim(q_all, keep_at, half, 1)

    core, x_hi = lax.rem(ta, 2), ta // 2
    width = out_weight.shape[1] // lax.axis_size("ta")
    ordered = jnp.concatenate(
        [lax.dynamic_slice_in_dim(out_weight, at, half, 0) for at in (keep_at, send_at)], axis=0
    )
    groups = (2 * (1 - x_hi) + 1 - core, 2 * (1 - x_hi) + core, 2 * x_hi + 1 - core, ta)
    weights = [lax.dynamic_slice_in_dim(ordered, group * width, width, 1) for group in groups]

    kv_pair = lax.ppermute(kv_send, "ha", swap_pairs)
    own_up, own_down = above_below(kv_own)
    far_p = lax.ppermute(kv_own, "ha", native_pairs)
    flags, *weights = lax.optimization_barrier((flags, *weights))
    state_n = attend(flags, q_own, [kv_own], [None])
    own_up, own_down, state_n = lax.optimization_barrier((own_up, own_down, state_n))
    far_p_rows = lax.ppermute(jnp.stack([own_up, own_down]), "ha", native_pairs)
    kv_pair, q_send, state_n, far_p = lax.optimization_barrier((kv_pair, q_send, state_n, far_p))
    q_pair = lax.ppermute(q_send, "ha", swap_pairs)
    pair_up, pair_down = above_below(kv_pair)
    far_n = lax.ppermute(kv_pair, "ha", swapped_pairs)

    state_n = attend(flags, q_own, [kv_pair, own_up, own_down], [None, 0, 1], state_n)
    q_pair, state_n = lax.optimization_barrier((q_pair, state_n))
    state_p = attend(flags, q_pair, [kv_own, kv_pair, own_up, own_down, far_p], [None, None, 0, 1, 2], cost=COST3)
    far_n, state_p = lax.optimization_barrier((far_n, state_p))
    far_n_up, far_n_down = above_below(far_n)
    state_p = attend(flags, q_pair, [pair_up, pair_down], [0, 1], state_p)
    state_n, state_p = lax.optimization_barrier((state_n, state_p))
    state_n = attend(flags, q_own, [pair_up, pair_down, far_n], [0, 1, 5], state_n)
    state_p, state_n = lax.optimization_barrier((state_p, state_n))
    backs = []
    for part in (0, 1):
        out_p = attend(
            flags, q_pair, [(far_p_rows, 0), (far_p_rows, 1)], [3, 4], state_p, last=True, part=part
        )
        state_p, state_n, out_p = lax.optimization_barrier((state_p, state_n, out_p))
        backs.append(lax.ppermute(out_p, "ha", swap_pairs))
    out_n = attend(flags, q_own, [far_n_up, far_n_down], [6, 7], state_n, last=True)
    back_0, back_1, out_n = lax.optimization_barrier((*backs, out_n))

    core_pairs = [(i, i ^ 1) for i in range(4)]
    hi_pairs = [(i, i ^ 2) for i in range(4)]

    attention = jnp.concatenate([out_n, jnp.concatenate([back_0, back_1], axis=0)], axis=1)

    def partial_of(group, start, stop):
        return jnp.dot(attention[start:stop], weights[group], preferred_element_type=jnp.float32)

    fars = []
    for start in (0, tokens // 2):
        stop = start + tokens // 2
        taken = lax.ppermute(partial_of(0, start, stop).astype(jnp.bfloat16), "ta", core_pairs)
        away = (partial_of(1, start, stop) + taken.astype(jnp.float32)).astype(jnp.bfloat16)
        fars.append(lax.ppermute(away, "ta", hi_pairs))
    home_taken = lax.ppermute(partial_of(2, 0, tokens).astype(jnp.bfloat16), "ta", core_pairs)
    home = partial_of(3, 0, tokens) + home_taken.astype(jnp.float32)
    result = home + jnp.concatenate(fars, axis=0).astype(jnp.float32)
    return result.astype(jnp.bfloat16).reshape(frames, rows, cols, width)


def solution(mesh):
    return jax.shard_map(
        body,
        mesh=mesh,
        in_specs=(P(None, "wa", "ha", "ta"), P(None, None, "wa", "ha", "ta"), P("ta", None)),
        out_specs=P(None, "wa", "ha", "ta"),
        check_vma=False,
    )
```

```python
import functools

import jax
import jax.numpy as jnp
from jax import lax
from jax.experimental import pallas as pl
from jax.experimental.pallas import tpu as pltpu
from jax.sharding import PartitionSpec as P

HD = 128
LOG2E = 1.4426950408889634
EXP_SCALE = HD ** (-0.5) * LOG2E
LOW = -1e30
LIMIT = 2.0**60
KEYS = 256


COST2 = 1024
COST3 = 32


def attend_kernel(gates, first, last, step, *refs):
    flags_ref, q_ref = refs[:2]
    tiles = refs[2 : 2 + len(gates)]
    rest = refs[2 + len(gates) :]
    if not first:
        acc_in, top_in = rest[:2]
        rest = rest[2:]
    tokens = q_ref.shape[0]
    span = tiles[0].shape[1]
    inside = [None if gate is None else flags_ref[gate] > 0 for gate in gates]
    ones = jnp.ones((span, HD), jnp.bfloat16)

    def scores_of(queries, tile, begin, size):
        return lax.dot_general(
            queries, tile[0, pl.ds(begin, size), :], (((1,), (1,)), ((), ())),
            preferred_element_type=jnp.float32,
        )

    def row_max(scores):
        return jnp.broadcast_to(jnp.max(scores, axis=1, keepdims=True), (scores.shape[0], HD))

    def weights_of(scores, shift):
        wide = jnp.concatenate([shift] * (scores.shape[1] // HD), axis=1)
        return jnp.exp2((scores - wide) * EXP_SCALE).astype(jnp.bfloat16)

    def store(rows, mixed, top):
        if last:
            rest[0][rows, :] = (mixed[:, :HD] / mixed[:, HD:]).astype(rest[0].dtype)
        else:
            rest[0][rows, :] = mixed
            rest[1][rows, :] = top

    def full_step(start, all_scores):
        rows = pl.ds(start, step)
        old = jnp.full((step, HD), LOW, jnp.float32) if first else top_in[rows, :]
        new = old
        for scores, valid in zip(all_scores, inside):
            largest = row_max(scores)
            new = jnp.maximum(new, largest if valid is None else jnp.where(valid, largest, LOW))
        mixed = None
        for scores, valid, tile in zip(all_scores, inside, tiles):
            weights = weights_of(scores, new if valid is None else jnp.where(valid, new, -LOW))
            values = jnp.concatenate([tile[1], ones], axis=1)
            part = jnp.dot(weights, values, preferred_element_type=jnp.float32)
            mixed = part if mixed is None else mixed + part
        if not first:
            keep = jnp.exp2((old - new) * EXP_SCALE)
            mixed = acc_in[rows, :] * jnp.concatenate([keep, keep], axis=1) + mixed
        store(rows, mixed, new)

    def tile_scores(start):
        queries = q_ref[pl.ds(start, step), :]
        return [scores_of(queries, tile, 0, span) for tile in tiles]

    if first:
        ready = tile_scores(0)
        for start in range(0, tokens, step):
            following = tile_scores(start + step) if start + step < tokens else None
            full_step(start, ready)
            ready = following
        return

    def quick_weights(start):
        rows = pl.ds(start, step)
        queries = q_ref[rows, :]
        top = top_in[rows, :]
        parts = []
        for tile, valid in zip(tiles, inside):
            shift = top if valid is None else jnp.where(valid, top, -LOW)
            for begin in range(0, span, KEYS):
                parts.append(weights_of(scores_of(queries, tile, begin, KEYS), shift))
        return jnp.concatenate(parts, axis=1), top

    values = jnp.concatenate([jnp.concatenate([tile[1], ones], axis=1) for tile in tiles], axis=0)
    totals = None
    ready = quick_weights(0)
    for start in range(0, tokens, step):
        following = quick_weights(start + step) if start + step < tokens else None
        rows = pl.ds(start, step)
        mixed = jnp.dot(ready[0], values, preferred_element_type=jnp.float32)
        total = mixed[:, HD:]
        totals = total if totals is None else jnp.maximum(totals, total)
        store(rows, acc_in[rows, :] + mixed, ready[1])
        ready = following

    @pl.when(jnp.logical_not(jnp.max(totals) < LIMIT))
    def _():
        for start in range(0, tokens, step):
            full_step(start, tile_scores(start))


def attend(flags, queries, tiles, gates, state=None, last=False, part=None, cost=32):
    channels = queries.shape[1]
    tokens = queries.shape[0] if part is None else queries.shape[0] // 2
    heads = channels // HD
    span = queries.shape[0]
    def rows_spec(array, width):
        block = 0 if part is None or array.shape[0] == tokens else part
        return pl.BlockSpec((tokens, width), lambda h: (block, h))

    tile_spec = pl.BlockSpec((2, span, HD), lambda h: (0, 0, h))
    in_specs = [pl.BlockSpec(memory_space=pltpu.SMEM), rows_spec(queries, HD)] + [tile_spec] * len(tiles)
    args = [flags, queries, *tiles]
    if state is not None:
        in_specs += [rows_spec(state[0], 2 * HD), rows_spec(state[1], HD)]
        args += list(state)
    if last:
        out_shape = jax.ShapeDtypeStruct((tokens, channels), jnp.bfloat16)
        out_specs = rows_spec(out_shape, HD)
    else:
        out_shape = [
            jax.ShapeDtypeStruct((tokens, 2 * channels), jnp.float32),
            jax.ShapeDtypeStruct((tokens, channels), jnp.float32),
        ]
        out_specs = [rows_spec(out_shape[0], 2 * HD), rows_spec(out_shape[1], HD)]
    step = 256 if tokens % 256 == 0 else 192
    pairs = len(tiles) * heads * tokens * span
    return pl.pallas_call(
        functools.partial(attend_kernel, tuple(gates), state is None, last, step),
        out_shape=out_shape,
        grid=(heads,),
        in_specs=in_specs,
        out_specs=out_specs,
        compiler_params=pltpu.CompilerParams(vmem_limit_bytes=28 * 1024 * 1024),
        cost_estimate=pl.CostEstimate(flops=pairs * cost, bytes_accessed=1024, transcendentals=0),
    )(*args)


def body(queries, keys_values, out_weight):
    frames, rows, cols, channels = queries.shape
    tokens = frames * rows * cols
    half = channels // 2
    ha_count, wa_count = lax.axis_size("ha"), lax.axis_size("wa")
    ha, wa, ta = lax.axis_index("ha"), lax.axis_index("wa"), lax.axis_index("ta")
    odd = lax.rem(ha, 2)

    q_all = queries.reshape(tokens, channels)
    kv_all = keys_values.reshape(2, tokens, channels)
    keep_at, send_at = odd * half, (1 - odd) * half

    swap_pairs = [(i, i ^ 1) for i in range(ha_count)]
    native_pairs = [(i, (i + (2 if i % 2 else -2)) % ha_count) for i in range(ha_count)]
    swapped_pairs = [(i, (i + (-2 if i % 2 else 2)) % ha_count) for i in range(ha_count)]
    down_pairs = [(i, (i + 1) % wa_count) for i in range(wa_count)]
    up_pairs = [((i + 1) % wa_count, i) for i in range(wa_count)]

    def above_below(cells):
        return lax.ppermute(cells, "wa", down_pairs), lax.ppermute(cells, "wa", up_pairs)

    above, below = wa > 0, wa < wa_count - 1
    low, high = ha >= 2, ha < ha_count - 2
    far_partner = jnp.where(odd == 1, low, high)
    far_native = jnp.where(odd == 1, high, low)
    flags = jnp.stack(
        [above, below, far_partner, far_partner & above, far_partner & below,
         far_native, far_native & above, far_native & below]
    ).astype(jnp.int32)

    kv_send = lax.dynamic_slice_in_dim(kv_all, send_at, half, 2)
    kv_send, kv_all = lax.optimization_barrier((kv_send, kv_all))
    kv_own = lax.dynamic_slice_in_dim(kv_all, keep_at, half, 2)
    q_send = lax.dynamic_slice_in_dim(q_all, send_at, half, 1)
    q_own = lax.dynamic_slice_in_dim(q_all, keep_at, half, 1)

    core, x_hi = lax.rem(ta, 2), ta // 2
    width = out_weight.shape[1] // lax.axis_size("ta")
    ordered = jnp.concatenate(
        [lax.dynamic_slice_in_dim(out_weight, at, half, 0) for at in (keep_at, send_at)], axis=0
    )
    groups = (2 * (1 - x_hi) + 1 - core, 2 * (1 - x_hi) + core, 2 * x_hi + 1 - core, ta)
    weights = [lax.dynamic_slice_in_dim(ordered, group * width, width, 1) for group in groups]

    kv_pair = lax.ppermute(kv_send, "ha", swap_pairs)
    own_up, own_down = above_below(kv_own)
    far_p = lax.ppermute(kv_own, "ha", native_pairs)
    weight_send = jnp.concatenate([weights[0], weights[2]], axis=1)
    weight_keep = jnp.concatenate([weights[1], weights[3]], axis=1)
    flags, weight_send, weight_keep = lax.optimization_barrier((flags, weight_send, weight_keep))
    state_n = attend(flags, q_own, [kv_own], [None])
    own_up, own_down, state_n = lax.optimization_barrier((own_up, own_down, state_n))
    far_p_up = lax.ppermute(own_up, "ha", native_pairs)
    kv_pair, q_send, state_n, far_p = lax.optimization_barrier((kv_pair, q_send, state_n, far_p))
    q_pair = lax.ppermute(q_send, "ha", swap_pairs)
    pair_up, pair_down = above_below(kv_pair)
    far_n = lax.ppermute(kv_pair, "ha", swapped_pairs)

    state_n = attend(flags, q_own, [kv_pair, own_up, own_down], [None, 0, 1], state_n)
    q_pair, state_n, own_down = lax.optimization_barrier((q_pair, state_n, own_down))
    far_p_down = lax.ppermute(own_down, "ha", native_pairs)
    state_p = attend(flags, q_pair, [kv_own, kv_pair, own_up, own_down, far_p], [None, None, 0, 1, 2], cost=COST3)
    far_n, state_p, far_p_up = lax.optimization_barrier((far_n, state_p, far_p_up))
    far_n_up, far_n_down = above_below(far_n)
    state_n, state_p = lax.optimization_barrier((state_n, state_p))
    state_n = attend(flags, q_own, [pair_up, pair_down, far_n], [0, 1, 5], state_n)
    state_p, state_n = lax.optimization_barrier((state_p, state_n))
    state_p = attend(flags, q_pair, [pair_up, pair_down, far_p_up], [0, 1, 3], state_p)
    state_p, state_n = lax.optimization_barrier((state_p, state_n))
    out_p = attend(flags, q_pair, [far_p_down], [4], state_p, last=True)
    state_n, out_p = lax.optimization_barrier((state_n, out_p))
    back = lax.ppermute(out_p, "ha", swap_pairs)
    out_n = attend(flags, q_own, [far_n_up, far_n_down], [6, 7], state_n, last=True)

    core_pairs = [(i, i ^ 1) for i in range(4)]
    hi_pairs = [(i, i ^ 2) for i in range(4)]

    attention = jnp.concatenate([out_n, back], axis=1)
    homes, fars = [], []
    for start in (0, tokens // 2):
        rows_here = attention[start : start + tokens // 2]
        sent = jnp.dot(rows_here, weight_send, preferred_element_type=jnp.float32).astype(jnp.bfloat16)
        taken = lax.ppermute(sent, "ta", core_pairs)
        kept = jnp.dot(rows_here, weight_keep, preferred_element_type=jnp.float32)
        away = (kept[:, :width] + taken[:, :width].astype(jnp.float32)).astype(jnp.bfloat16)
        away, attention = lax.optimization_barrier((away, attention))
        fars.append(lax.ppermute(away, "ta", hi_pairs))
        homes.append(kept[:, width:] + taken[:, width:].astype(jnp.float32))
    result = jnp.concatenate(
        [home + far.astype(jnp.float32) for home, far in zip(homes, fars)], axis=0
    )
    return result.astype(jnp.bfloat16).reshape(frames, rows, cols, width)


def solution(mesh):
    return jax.shard_map(
        body,
        mesh=mesh,
        in_specs=(P(None, "wa", "ha", "ta"), P(None, None, "wa", "ha", "ta"), P("ta", None)),
        out_specs=P(None, "wa", "ha", "ta"),
        check_vma=False,
    )
```

```python
import functools

import jax
import jax.numpy as jnp
from jax import lax
from jax.experimental import pallas as pl
from jax.experimental.pallas import tpu as pltpu
from jax.sharding import PartitionSpec as P

HD = 128
LOG2E = 1.4426950408889634
EXP_SCALE = HD ** (-0.5) * LOG2E
LOW = -1e30
LIMIT = 2.0**60
KEYS = 256


COST2 = 1024
COST3 = 32


def attend_kernel(gates, first, last, step, *refs):
    flags_ref, q_ref = refs[:2]
    tiles = refs[2 : 2 + len(gates)]
    rest = refs[2 + len(gates) :]
    if not first:
        acc_in, top_in = rest[:2]
        rest = rest[2:]
    tokens = q_ref.shape[0]
    span = tiles[0].shape[1]
    inside = [None if gate is None else flags_ref[gate] > 0 for gate in gates]
    ones = jnp.ones((span, HD), jnp.bfloat16)

    def scores_of(queries, tile, begin, size):
        return lax.dot_general(
            queries, tile[0, pl.ds(begin, size), :], (((1,), (1,)), ((), ())),
            preferred_element_type=jnp.float32,
        )

    def row_max(scores):
        return jnp.broadcast_to(jnp.max(scores, axis=1, keepdims=True), (scores.shape[0], HD))

    def weights_of(scores, shift):
        wide = jnp.concatenate([shift] * (scores.shape[1] // HD), axis=1)
        return jnp.exp2((scores - wide) * EXP_SCALE).astype(jnp.bfloat16)

    def store(rows, mixed, top):
        if last:
            rest[0][rows, :] = (mixed[:, :HD] / mixed[:, HD:]).astype(rest[0].dtype)
        else:
            rest[0][rows, :] = mixed
            rest[1][rows, :] = top

    def full_step(start, all_scores):
        rows = pl.ds(start, step)
        old = jnp.full((step, HD), LOW, jnp.float32) if first else top_in[rows, :]
        new = old
        for scores, valid in zip(all_scores, inside):
            largest = row_max(scores)
            new = jnp.maximum(new, largest if valid is None else jnp.where(valid, largest, LOW))
        mixed = None
        for scores, valid, tile in zip(all_scores, inside, tiles):
            weights = weights_of(scores, new if valid is None else jnp.where(valid, new, -LOW))
            values = jnp.concatenate([tile[1], ones], axis=1)
            part = jnp.dot(weights, values, preferred_element_type=jnp.float32)
            mixed = part if mixed is None else mixed + part
        if not first:
            keep = jnp.exp2((old - new) * EXP_SCALE)
            mixed = acc_in[rows, :] * jnp.concatenate([keep, keep], axis=1) + mixed
        store(rows, mixed, new)

    def tile_scores(start):
        queries = q_ref[pl.ds(start, step), :]
        return [scores_of(queries, tile, 0, span) for tile in tiles]

    if first:
        ready = tile_scores(0)
        for start in range(0, tokens, step):
            following = tile_scores(start + step) if start + step < tokens else None
            full_step(start, ready)
            ready = following
        return

    def quick_weights(start):
        rows = pl.ds(start, step)
        queries = q_ref[rows, :]
        top = top_in[rows, :]
        parts = []
        for tile, valid in zip(tiles, inside):
            shift = top if valid is None else jnp.where(valid, top, -LOW)
            for begin in range(0, span, KEYS):
                parts.append(weights_of(scores_of(queries, tile, begin, KEYS), shift))
        return jnp.concatenate(parts, axis=1), top

    values = jnp.concatenate([jnp.concatenate([tile[1], ones], axis=1) for tile in tiles], axis=0)
    totals = None
    ready = quick_weights(0)
    for start in range(0, tokens, step):
        following = quick_weights(start + step) if start + step < tokens else None
        rows = pl.ds(start, step)
        mixed = jnp.dot(ready[0], values, preferred_element_type=jnp.float32)
        total = mixed[:, HD:]
        totals = total if totals is None else jnp.maximum(totals, total)
        store(rows, acc_in[rows, :] + mixed, ready[1])
        ready = following

    @pl.when(jnp.logical_not(jnp.max(totals) < LIMIT))
    def _():
        for start in range(0, tokens, step):
            full_step(start, tile_scores(start))


def attend(flags, queries, tiles, gates, state=None, last=False, part=None, cost=32):
    channels = queries.shape[1]
    tokens = queries.shape[0] if part is None else queries.shape[0] // 2
    heads = channels // HD
    span = queries.shape[0]
    arrays = [tile[0] if isinstance(tile, tuple) else tile for tile in tiles]

    def tile_spec(tile):
        if isinstance(tile, tuple):
            return pl.BlockSpec((None, 2, span, HD), lambda h: (tile[1], 0, 0, h))
        return pl.BlockSpec((2, span, HD), lambda h: (0, 0, h))

    def rows_spec(array, width):
        block = 0 if part is None or array.shape[0] == tokens else part
        return pl.BlockSpec((tokens, width), lambda h: (block, h))

    in_specs = [pl.BlockSpec(memory_space=pltpu.SMEM), rows_spec(queries, HD)] + [tile_spec(tile) for tile in tiles]
    args = [flags, queries, *arrays]
    if state is not None:
        in_specs += [rows_spec(state[0], 2 * HD), rows_spec(state[1], HD)]
        args += list(state)
    if last:
        out_shape = jax.ShapeDtypeStruct((tokens, channels), jnp.bfloat16)
        out_specs = rows_spec(out_shape, HD)
    else:
        out_shape = [
            jax.ShapeDtypeStruct((tokens, 2 * channels), jnp.float32),
            jax.ShapeDtypeStruct((tokens, channels), jnp.float32),
        ]
        out_specs = [rows_spec(out_shape[0], 2 * HD), rows_spec(out_shape[1], HD)]
    step = 256 if tokens % 256 == 0 else 192
    pairs = len(tiles) * heads * tokens * span
    return pl.pallas_call(
        functools.partial(attend_kernel, tuple(gates), state is None, last, step),
        out_shape=out_shape,
        grid=(heads,),
        in_specs=in_specs,
        out_specs=out_specs,
        compiler_params=pltpu.CompilerParams(vmem_limit_bytes=28 * 1024 * 1024),
        cost_estimate=pl.CostEstimate(flops=pairs * cost, bytes_accessed=1024, transcendentals=0),
    )(*args)


def body(queries, keys_values, out_weight):
    frames, rows, cols, channels = queries.shape
    tokens = frames * rows * cols
    half = channels // 2
    ha_count, wa_count = lax.axis_size("ha"), lax.axis_size("wa")
    ha, wa, ta = lax.axis_index("ha"), lax.axis_index("wa"), lax.axis_index("ta")
    odd = lax.rem(ha, 2)

    q_all = queries.reshape(tokens, channels)
    kv_all = keys_values.reshape(2, tokens, channels)
    keep_at, send_at = odd * half, (1 - odd) * half

    swap_pairs = [(i, i ^ 1) for i in range(ha_count)]
    native_pairs = [(i, (i + (2 if i % 2 else -2)) % ha_count) for i in range(ha_count)]
    swapped_pairs = [(i, (i + (-2 if i % 2 else 2)) % ha_count) for i in range(ha_count)]
    down_pairs = [(i, (i + 1) % wa_count) for i in range(wa_count)]
    up_pairs = [((i + 1) % wa_count, i) for i in range(wa_count)]

    def above_below(cells):
        return lax.ppermute(cells, "wa", down_pairs), lax.ppermute(cells, "wa", up_pairs)

    above, below = wa > 0, wa < wa_count - 1
    low, high = ha >= 2, ha < ha_count - 2
    far_partner = jnp.where(odd == 1, low, high)
    far_native = jnp.where(odd == 1, high, low)
    flags = jnp.stack(
        [above, below, far_partner, far_partner & above, far_partner & below,
         far_native, far_native & above, far_native & below]
    ).astype(jnp.int32)

    kv_send = lax.dynamic_slice_in_dim(kv_all, send_at, half, 2)
    kv_send, kv_all = lax.optimization_barrier((kv_send, kv_all))
    kv_own = lax.dynamic_slice_in_dim(kv_all, keep_at, half, 2)
    q_send = lax.dynamic_slice_in_dim(q_all, send_at, half, 1)
    q_own = lax.dynamic_slice_in_dim(q_all, keep_at, half, 1)

    width = out_weight.shape[1] // lax.axis_size("ta")
    core_pairs = [(i, i ^ 1) for i in range(4)]
    across = ("ha", "ta")

    def across_pairs(ha_flip, ta_flip):
        return [(i, i ^ (4 * ha_flip + ta_flip)) for i in range(4 * ha_count)]

    def weight_for(weight, group):
        return lax.dynamic_slice_in_dim(weight, group * width, width, 1)

    kv_pair = lax.ppermute(kv_send, "ha", swap_pairs)
    own_up, own_down = above_below(kv_own)
    far_p = lax.ppermute(kv_own, "ha", native_pairs)
    weight_hi = lax.ppermute(weight_for(out_weight, ta ^ 2), across, across_pairs(1, 2))
    state_n = attend(flags, q_own, [kv_own], [None])
    own_up, own_down, state_n = lax.optimization_barrier((own_up, own_down, state_n))
    far_p_rows = lax.ppermute(jnp.stack([own_up, own_down]), "ha", native_pairs)
    kv_pair, q_send, state_n, far_p = lax.optimization_barrier((kv_pair, q_send, state_n, far_p))
    flags, weight_hi = lax.optimization_barrier((flags, weight_hi))
    q_pair = lax.ppermute(q_send, "ha", swap_pairs)
    pair_up, pair_down = above_below(kv_pair)
    far_n = lax.ppermute(kv_pair, "ha", swapped_pairs)

    state_n = attend(flags, q_own, [kv_pair, own_up, own_down], [None, 0, 1], state_n)
    q_pair, state_n, late = lax.optimization_barrier((q_pair, state_n, ta))
    weight_hi_core = lax.ppermute(weight_for(out_weight, late ^ 3), across, across_pairs(1, 3))
    state_p = attend(flags, q_pair, [kv_own, kv_pair, own_up, own_down, far_p], [None, None, 0, 1, 2], cost=COST3)
    far_n, state_p, late = lax.optimization_barrier((far_n, state_p, late))
    far_n_up, far_n_down = above_below(far_n)
    state_p = attend(flags, q_pair, [pair_up, pair_down], [0, 1], state_p)
    state_n, state_p = lax.optimization_barrier((state_n, state_p))
    state_n = attend(flags, q_own, [pair_up, pair_down, far_n], [0, 1, 5], state_n)
    state_p, state_n = lax.optimization_barrier((state_p, state_n))
    flags, weight_hi_core = lax.optimization_barrier((flags, weight_hi_core))
    out_p = attend(flags, q_pair, [(far_p_rows, 0), (far_p_rows, 1)], [3, 4], state_p, last=True)
    state_n, out_p, late = lax.optimization_barrier((state_n, out_p, late))
    back = lax.ppermute(out_p, "ha", swap_pairs)
    back_hi = lax.ppermute(out_p, across, across_pairs(1, 2))
    weight_core = lax.ppermute(weight_for(out_weight, late ^ 1), "ta", core_pairs)
    out_n = attend(flags, q_own, [far_n_up, far_n_down], [6, 7], state_n, last=True)
    out_hi = lax.ppermute(out_n, "ta", [(i, i ^ 2) for i in range(4)])

    def product(cells, weight, at):
        rows_here = lax.dynamic_slice_in_dim(weight, at, half, 0)
        return jnp.dot(cells, rows_here, preferred_element_type=jnp.float32)

    weight_own = weight_for(out_weight, ta)
    total = None
    for cells, weight, weight_other, at in (
        (out_n, weight_own, weight_core, keep_at),
        (back, weight_own, weight_core, send_at),
        (back_hi, weight_hi, weight_hi_core, send_at),
        (out_hi, weight_hi, weight_hi_core, keep_at),
    ):
        other = lax.ppermute(cells, "ta", core_pairs)
        part = product(cells, weight, at) + product(other, weight_other, at)
        total = part if total is None else total + part
    return total.astype(jnp.bfloat16).reshape(frames, rows, cols, width)


def solution(mesh):
    return jax.shard_map(
        body,
        mesh=mesh,
        in_specs=(P(None, "wa", "ha", "ta"), P(None, None, "wa", "ha", "ta"), P("ta", None)),
        out_specs=P(None, "wa", "ha", "ta"),
        check_vma=False,
    )
```

```python
import functools

import jax
import jax.numpy as jnp
from jax import lax
from jax.experimental import pallas as pl
from jax.experimental.pallas import tpu as pltpu
from jax.sharding import PartitionSpec as P

HD = 128
LOG2E = 1.4426950408889634
EXP_SCALE = HD ** (-0.5) * LOG2E
LOW = -1e30
LIMIT = 2.0**60
KEYS = 256


COST2 = 1024
COST3 = 32


def attend_kernel(gates, first, last, step, *refs):
    flags_ref, q_ref = refs[:2]
    tiles = refs[2 : 2 + len(gates)]
    rest = refs[2 + len(gates) :]
    if not first:
        acc_in, top_in = rest[:2]
        rest = rest[2:]
    tokens = q_ref.shape[0]
    span = tiles[0].shape[1]
    inside = [None if gate is None else flags_ref[gate] > 0 for gate in gates]
    ones = jnp.ones((span, HD), jnp.bfloat16)

    def scores_of(queries, tile, begin, size):
        return lax.dot_general(
            queries, tile[0, pl.ds(begin, size), :], (((1,), (1,)), ((), ())),
            preferred_element_type=jnp.float32,
        )

    def row_max(scores):
        return jnp.broadcast_to(jnp.max(scores, axis=1, keepdims=True), (scores.shape[0], HD))

    def weights_of(scores, shift):
        wide = jnp.concatenate([shift] * (scores.shape[1] // HD), axis=1)
        return jnp.exp2((scores - wide) * EXP_SCALE).astype(jnp.bfloat16)

    def store(rows, mixed, top):
        if last:
            rest[0][rows, :] = (mixed[:, :HD] / mixed[:, HD:]).astype(rest[0].dtype)
        else:
            rest[0][rows, :] = mixed
            rest[1][rows, :] = top

    def full_step(start, all_scores):
        rows = pl.ds(start, step)
        old = jnp.full((step, HD), LOW, jnp.float32) if first else top_in[rows, :]
        new = old
        for scores, valid in zip(all_scores, inside):
            largest = row_max(scores)
            new = jnp.maximum(new, largest if valid is None else jnp.where(valid, largest, LOW))
        mixed = None
        for scores, valid, tile in zip(all_scores, inside, tiles):
            weights = weights_of(scores, new if valid is None else jnp.where(valid, new, -LOW))
            values = jnp.concatenate([tile[1], ones], axis=1)
            part = jnp.dot(weights, values, preferred_element_type=jnp.float32)
            mixed = part if mixed is None else mixed + part
        if not first:
            keep = jnp.exp2((old - new) * EXP_SCALE)
            mixed = acc_in[rows, :] * jnp.concatenate([keep, keep], axis=1) + mixed
        store(rows, mixed, new)

    def tile_scores(start):
        queries = q_ref[pl.ds(start, step), :]
        return [scores_of(queries, tile, 0, span) for tile in tiles]

    if first:
        ready = tile_scores(0)
        for start in range(0, tokens, step):
            following = tile_scores(start + step) if start + step < tokens else None
            full_step(start, ready)
            ready = following
        return

    def quick_weights(start):
        rows = pl.ds(start, step)
        queries = q_ref[rows, :]
        top = top_in[rows, :]
        parts = []
        for tile, valid in zip(tiles, inside):
            shift = top if valid is None else jnp.where(valid, top, -LOW)
            for begin in range(0, span, KEYS):
                parts.append(weights_of(scores_of(queries, tile, begin, KEYS), shift))
        return jnp.concatenate(parts, axis=1), top

    values = jnp.concatenate([jnp.concatenate([tile[1], ones], axis=1) for tile in tiles], axis=0)
    totals = None
    ready = quick_weights(0)
    for start in range(0, tokens, step):
        following = quick_weights(start + step) if start + step < tokens else None
        rows = pl.ds(start, step)
        mixed = jnp.dot(ready[0], values, preferred_element_type=jnp.float32)
        total = mixed[:, HD:]
        totals = total if totals is None else jnp.maximum(totals, total)
        store(rows, acc_in[rows, :] + mixed, ready[1])
        ready = following

    @pl.when(jnp.logical_not(jnp.max(totals) < LIMIT))
    def _():
        for start in range(0, tokens, step):
            full_step(start, tile_scores(start))


def attend(flags, queries, tiles, gates, state=None, last=False, part=None, cost=32):
    channels = queries.shape[1]
    tokens = queries.shape[0] if part is None else queries.shape[0] // 2
    heads = channels // HD
    span = queries.shape[0]
    arrays = [tile[0] if isinstance(tile, tuple) else tile for tile in tiles]

    def tile_spec(tile):
        if isinstance(tile, tuple):
            return pl.BlockSpec((None, 2, span, HD), lambda h: (tile[1], 0, 0, h))
        return pl.BlockSpec((2, span, HD), lambda h: (0, 0, h))

    def rows_spec(array, width):
        block = 0 if part is None or array.shape[0] == tokens else part
        return pl.BlockSpec((tokens, width), lambda h: (block, h))

    in_specs = [pl.BlockSpec(memory_space=pltpu.SMEM), rows_spec(queries, HD)] + [tile_spec(tile) for tile in tiles]
    args = [flags, queries, *arrays]
    if state is not None:
        in_specs += [rows_spec(state[0], 2 * HD), rows_spec(state[1], HD)]
        args += list(state)
    if last:
        out_shape = jax.ShapeDtypeStruct((tokens, channels), jnp.bfloat16)
        out_specs = rows_spec(out_shape, HD)
    else:
        out_shape = [
            jax.ShapeDtypeStruct((tokens, 2 * channels), jnp.float32),
            jax.ShapeDtypeStruct((tokens, channels), jnp.float32),
        ]
        out_specs = [rows_spec(out_shape[0], 2 * HD), rows_spec(out_shape[1], HD)]
    step = 256 if tokens % 256 == 0 else 192
    pairs = len(tiles) * heads * tokens * span
    return pl.pallas_call(
        functools.partial(attend_kernel, tuple(gates), state is None, last, step),
        out_shape=out_shape,
        grid=(heads,),
        in_specs=in_specs,
        out_specs=out_specs,
        compiler_params=pltpu.CompilerParams(vmem_limit_bytes=28 * 1024 * 1024),
        cost_estimate=pl.CostEstimate(flops=pairs * cost, bytes_accessed=1024, transcendentals=0),
    )(*args)


def body(queries, keys_values, out_weight):
    frames, rows, cols, channels = queries.shape
    tokens = frames * rows * cols
    half = channels // 2
    ha_count, wa_count = lax.axis_size("ha"), lax.axis_size("wa")
    ha, wa, ta = lax.axis_index("ha"), lax.axis_index("wa"), lax.axis_index("ta")
    odd = lax.rem(ha, 2)

    q_all = queries.reshape(tokens, channels)
    kv_all = keys_values.reshape(2, tokens, channels)
    keep_at, send_at = odd * half, (1 - odd) * half

    swap_pairs = [(i, i ^ 1) for i in range(ha_count)]
    native_pairs = [(i, (i + (2 if i % 2 else -2)) % ha_count) for i in range(ha_count)]
    swapped_pairs = [(i, (i + (-2 if i % 2 else 2)) % ha_count) for i in range(ha_count)]
    down_pairs = [(i, (i + 1) % wa_count) for i in range(wa_count)]
    up_pairs = [((i + 1) % wa_count, i) for i in range(wa_count)]

    def above_below(cells):
        return lax.ppermute(cells, "wa", down_pairs), lax.ppermute(cells, "wa", up_pairs)

    above, below = wa > 0, wa < wa_count - 1
    low, high = ha >= 2, ha < ha_count - 2
    far_partner = jnp.where(odd == 1, low, high)
    far_native = jnp.where(odd == 1, high, low)
    flags = jnp.stack(
        [above, below, far_partner, far_partner & above, far_partner & below,
         far_native, far_native & above, far_native & below]
    ).astype(jnp.int32)

    kv_send = lax.dynamic_slice_in_dim(kv_all, send_at, half, 2)
    kv_send, kv_all = lax.optimization_barrier((kv_send, kv_all))
    kv_own = lax.dynamic_slice_in_dim(kv_all, keep_at, half, 2)
    q_send = lax.dynamic_slice_in_dim(q_all, send_at, half, 1)
    q_own = lax.dynamic_slice_in_dim(q_all, keep_at, half, 1)

    width = out_weight.shape[1] // lax.axis_size("ta")
    core_pairs = [(i, i ^ 1) for i in range(4)]
    across = ("ha", "ta")

    def across_pairs(ha_flip, ta_flip):
        return [(i, i ^ (4 * ha_flip + ta_flip)) for i in range(4 * ha_count)]

    def weight_for(weight, group):
        return lax.dynamic_slice_in_dim(weight, group * width, width, 1)

    kv_pair = lax.ppermute(kv_send, "ha", swap_pairs)
    own_up, own_down = above_below(kv_own)
    far_p = lax.ppermute(kv_own, "ha", native_pairs)
    weight_hi = lax.ppermute(weight_for(out_weight, ta ^ 2), across, across_pairs(1, 2))
    state_n = attend(flags, q_own, [kv_own], [None])
    own_up, own_down, state_n = lax.optimization_barrier((own_up, own_down, state_n))
    far_p_rows = lax.ppermute(jnp.stack([own_up, own_down]), "ha", native_pairs)
    kv_pair, q_send, state_n, far_p = lax.optimization_barrier((kv_pair, q_send, state_n, far_p))
    flags, weight_hi = lax.optimization_barrier((flags, weight_hi))
    q_pair = lax.ppermute(q_send, "ha", swap_pairs)
    pair_up, pair_down = above_below(kv_pair)
    far_n = lax.ppermute(kv_pair, "ha", swapped_pairs)

    state_n = attend(flags, q_own, [kv_pair, own_up, own_down], [None, 0, 1], state_n)
    q_pair, state_n = lax.optimization_barrier((q_pair, state_n))
    state_p = attend(flags, q_pair, [kv_own, kv_pair, own_up, own_down, far_p], [None, None, 0, 1, 2], cost=COST3)
    far_n, state_p, late = lax.optimization_barrier((far_n, state_p, ta))
    far_n_up, far_n_down = above_below(far_n)
    weight_hi_core = lax.ppermute(weight_for(out_weight, late ^ 3), across, across_pairs(1, 3))
    state_p = attend(flags, q_pair, [pair_up, pair_down], [0, 1], state_p)
    state_n, state_p = lax.optimization_barrier((state_n, state_p))
    state_n = attend(flags, q_own, [pair_up, pair_down, far_n], [0, 1, 5], state_n)
    state_p, state_n = lax.optimization_barrier((state_p, state_n))
    flags, weight_hi_core = lax.optimization_barrier((flags, weight_hi_core))
    out_p = attend(flags, q_pair, [(far_p_rows, 0), (far_p_rows, 1)], [3, 4], state_p, last=True)
    state_n, out_p, late = lax.optimization_barrier((state_n, out_p, late))
    back = lax.ppermute(out_p, "ha", swap_pairs)
    back_hi = lax.ppermute(out_p, across, across_pairs(1, 2))
    weight_core = lax.ppermute(weight_for(out_weight, late ^ 1), "ta", core_pairs)
    out_n = attend(flags, q_own, [far_n_up, far_n_down], [6, 7], state_n, last=True)
    out_hi = lax.ppermute(out_n, "ta", [(i, i ^ 2) for i in range(4)])

    weight_own = weight_for(out_weight, late)

    def product(left, weight, rows_at):
        rows_here = lax.dynamic_slice_in_dim(weight, rows_at, half, 0)
        return jnp.dot(left, rows_here, preferred_element_type=jnp.float32)

    def other(cells):
        return lax.ppermute(cells, "ta", core_pairs)

    out_other, back_other, back_hi_other = other(out_n), other(back), other(back_hi)
    early = product(out_n, weight_own, keep_at) + product(back, weight_own, send_at)
    early = early + product(back_hi, weight_hi, send_at)
    early, out_hi, out_other = lax.optimization_barrier((early, out_hi, out_other))
    total = early + product(out_other, weight_core, keep_at) + product(back_other, weight_core, send_at)
    total = total + product(back_hi_other, weight_hi_core, send_at)
    total = total + product(out_hi, weight_hi, keep_at) + product(other(out_hi), weight_hi_core, keep_at)
    return total.astype(jnp.bfloat16).reshape(frames, rows, cols, width)


def solution(mesh):
    return jax.shard_map(
        body,
        mesh=mesh,
        in_specs=(P(None, "wa", "ha", "ta"), P(None, None, "wa", "ha", "ta"), P("ta", None)),
        out_specs=P(None, "wa", "ha", "ta"),
        check_vma=False,
    )
```

```python
import functools

import jax
import jax.numpy as jnp
from jax import lax
from jax.experimental import pallas as pl
from jax.experimental.pallas import tpu as pltpu
from jax.sharding import PartitionSpec as P

HD = 128
LOG2E = 1.4426950408889634
EXP_SCALE = HD ** (-0.5) * LOG2E
LOW = -1e30
LIMIT = 2.0**60
KEYS = 256


COST2 = 1024
COST3 = 32


def attend_kernel(gates, first, last, step, *refs):
    flags_ref, q_ref = refs[:2]
    tiles = refs[2 : 2 + len(gates)]
    rest = refs[2 + len(gates) :]
    if not first:
        acc_in, top_in = rest[:2]
        rest = rest[2:]
    tokens = q_ref.shape[0]
    span = tiles[0].shape[1]
    inside = [None if gate is None else flags_ref[gate] > 0 for gate in gates]
    ones = jnp.ones((span, HD), jnp.bfloat16)

    def scores_of(queries, tile, begin, size):
        return lax.dot_general(
            queries, tile[0, pl.ds(begin, size), :], (((1,), (1,)), ((), ())),
            preferred_element_type=jnp.float32,
        )

    def row_max(scores):
        return jnp.broadcast_to(jnp.max(scores, axis=1, keepdims=True), (scores.shape[0], HD))

    def weights_of(scores, shift):
        wide = jnp.concatenate([shift] * (scores.shape[1] // HD), axis=1)
        return jnp.exp2((scores - wide) * EXP_SCALE).astype(jnp.bfloat16)

    def store(rows, mixed, top):
        if last:
            rest[0][rows, :] = (mixed[:, :HD] / mixed[:, HD:]).astype(rest[0].dtype)
        else:
            rest[0][rows, :] = mixed
            rest[1][rows, :] = top

    def full_step(start, all_scores):
        rows = pl.ds(start, step)
        old = jnp.full((step, HD), LOW, jnp.float32) if first else top_in[rows, :]
        new = old
        for scores, valid in zip(all_scores, inside):
            largest = row_max(scores)
            new = jnp.maximum(new, largest if valid is None else jnp.where(valid, largest, LOW))
        mixed = None
        for scores, valid, tile in zip(all_scores, inside, tiles):
            weights = weights_of(scores, new if valid is None else jnp.where(valid, new, -LOW))
            values = jnp.concatenate([tile[1], ones], axis=1)
            part = jnp.dot(weights, values, preferred_element_type=jnp.float32)
            mixed = part if mixed is None else mixed + part
        if not first:
            keep = jnp.exp2((old - new) * EXP_SCALE)
            mixed = acc_in[rows, :] * jnp.concatenate([keep, keep], axis=1) + mixed
        store(rows, mixed, new)

    def tile_scores(start):
        queries = q_ref[pl.ds(start, step), :]
        return [scores_of(queries, tile, 0, span) for tile in tiles]

    if first:
        ready = tile_scores(0)
        for start in range(0, tokens, step):
            following = tile_scores(start + step) if start + step < tokens else None
            full_step(start, ready)
            ready = following
        return

    def quick_weights(start):
        rows = pl.ds(start, step)
        queries = q_ref[rows, :]
        top = top_in[rows, :]
        parts = []
        for tile, valid in zip(tiles, inside):
            shift = top if valid is None else jnp.where(valid, top, -LOW)
            for begin in range(0, span, KEYS):
                parts.append(weights_of(scores_of(queries, tile, begin, KEYS), shift))
        return jnp.concatenate(parts, axis=1), top

    values = jnp.concatenate([jnp.concatenate([tile[1], ones], axis=1) for tile in tiles], axis=0)
    totals = None
    ready = quick_weights(0)
    for start in range(0, tokens, step):
        following = quick_weights(start + step) if start + step < tokens else None
        rows = pl.ds(start, step)
        mixed = jnp.dot(ready[0], values, preferred_element_type=jnp.float32)
        total = mixed[:, HD:]
        totals = total if totals is None else jnp.maximum(totals, total)
        store(rows, acc_in[rows, :] + mixed, ready[1])
        ready = following

    @pl.when(jnp.logical_not(jnp.max(totals) < LIMIT))
    def _():
        @pl.loop(0, tokens // step)
        def _(index):
            start = pl.multiple_of(index * step, step)
            full_step(start, tile_scores(start))


def attend(flags, queries, tiles, gates, state=None, last=False, part=None, cost=32):
    channels = queries.shape[1]
    tokens = queries.shape[0] if part is None else queries.shape[0] // 2
    heads = channels // HD
    span = queries.shape[0]
    arrays = [tile[0] if isinstance(tile, tuple) else tile for tile in tiles]

    def tile_spec(tile):
        if isinstance(tile, tuple):
            return pl.BlockSpec((None, 2, span, HD), lambda h: (tile[1], 0, 0, h))
        return pl.BlockSpec((2, span, HD), lambda h: (0, 0, h))

    def rows_spec(array, width):
        block = 0 if part is None or array.shape[0] == tokens else part
        return pl.BlockSpec((tokens, width), lambda h: (block, h))

    in_specs = [pl.BlockSpec(memory_space=pltpu.SMEM), rows_spec(queries, HD)] + [tile_spec(tile) for tile in tiles]
    args = [flags, queries, *arrays]
    if state is not None:
        in_specs += [rows_spec(state[0], 2 * HD), rows_spec(state[1], HD)]
        args += list(state)
    if last:
        out_shape = jax.ShapeDtypeStruct((tokens, channels), jnp.bfloat16)
        out_specs = rows_spec(out_shape, HD)
    else:
        out_shape = [
            jax.ShapeDtypeStruct((tokens, 2 * channels), jnp.float32),
            jax.ShapeDtypeStruct((tokens, channels), jnp.float32),
        ]
        out_specs = [rows_spec(out_shape[0], 2 * HD), rows_spec(out_shape[1], HD)]
    step = 256 if tokens % 256 == 0 else 192
    pairs = len(tiles) * heads * tokens * span
    return pl.pallas_call(
        functools.partial(attend_kernel, tuple(gates), state is None, last, step),
        out_shape=out_shape,
        grid=(heads,),
        in_specs=in_specs,
        out_specs=out_specs,
        compiler_params=pltpu.CompilerParams(vmem_limit_bytes=28 * 1024 * 1024),
        cost_estimate=pl.CostEstimate(flops=pairs * cost, bytes_accessed=1024, transcendentals=0),
    )(*args)


def body(queries, keys_values, out_weight):
    frames, rows, cols, channels = queries.shape
    tokens = frames * rows * cols
    half = channels // 2
    ha_count, wa_count = lax.axis_size("ha"), lax.axis_size("wa")
    ha, wa, ta = lax.axis_index("ha"), lax.axis_index("wa"), lax.axis_index("ta")
    odd = lax.rem(ha, 2)

    q_all = queries.reshape(tokens, channels)
    kv_all = keys_values.reshape(2, tokens, channels)
    keep_at, send_at = odd * half, (1 - odd) * half

    swap_pairs = [(i, i ^ 1) for i in range(ha_count)]
    native_pairs = [(i, (i + (2 if i % 2 else -2)) % ha_count) for i in range(ha_count)]
    swapped_pairs = [(i, (i + (-2 if i % 2 else 2)) % ha_count) for i in range(ha_count)]
    down_pairs = [(i, (i + 1) % wa_count) for i in range(wa_count)]
    up_pairs = [((i + 1) % wa_count, i) for i in range(wa_count)]

    def above_below(cells):
        return lax.ppermute(cells, "wa", down_pairs), lax.ppermute(cells, "wa", up_pairs)

    above, below = wa > 0, wa < wa_count - 1
    low, high = ha >= 2, ha < ha_count - 2
    far_partner = jnp.where(odd == 1, low, high)
    far_native = jnp.where(odd == 1, high, low)
    flags = jnp.stack(
        [above, below, far_partner, far_partner & above, far_partner & below,
         far_native, far_native & above, far_native & below]
    ).astype(jnp.int32)

    kv_send = lax.dynamic_slice_in_dim(kv_all, send_at, half, 2)
    kv_send, kv_all = lax.optimization_barrier((kv_send, kv_all))
    kv_own = lax.dynamic_slice_in_dim(kv_all, keep_at, half, 2)
    q_send = lax.dynamic_slice_in_dim(q_all, send_at, half, 1)
    q_own = lax.dynamic_slice_in_dim(q_all, keep_at, half, 1)

    core, x_hi = lax.rem(ta, 2), ta // 2
    width = out_weight.shape[1] // lax.axis_size("ta")
    ordered = jnp.concatenate(
        [lax.dynamic_slice_in_dim(out_weight, at, half, 0) for at in (keep_at, send_at)], axis=0
    )
    groups = (2 * (1 - x_hi) + 1 - core, 2 * (1 - x_hi) + core, 2 * x_hi + 1 - core, ta)
    weights = [lax.dynamic_slice_in_dim(ordered, group * width, width, 1) for group in groups]

    kv_pair = lax.ppermute(kv_send, "ha", swap_pairs)
    own_up, own_down = above_below(kv_own)
    far_p = lax.ppermute(kv_own, "ha", native_pairs)
    flags, *weights = lax.optimization_barrier((flags, *weights))
    state_n = attend(flags, q_own, [kv_own], [None])
    own_up, own_down, state_n = lax.optimization_barrier((own_up, own_down, state_n))
    far_p_rows = lax.ppermute(jnp.stack([own_up, own_down]), "ha", native_pairs)
    kv_pair, q_send, state_n, far_p = lax.optimization_barrier((kv_pair, q_send, state_n, far_p))
    q_pair = lax.ppermute(q_send, "ha", swap_pairs)
    pair_up, pair_down = above_below(kv_pair)
    far_n = lax.ppermute(kv_pair, "ha", swapped_pairs)

    state_n = attend(flags, q_own, [kv_pair, own_up, own_down], [None, 0, 1], state_n)
    q_pair, state_n = lax.optimization_barrier((q_pair, state_n))
    state_p = attend(flags, q_pair, [kv_own, kv_pair, own_up, own_down, far_p], [None, None, 0, 1, 2], cost=COST3)
    far_n, state_p = lax.optimization_barrier((far_n, state_p))
    far_n_up, far_n_down = above_below(far_n)
    state_p = attend(flags, q_pair, [pair_up, pair_down], [0, 1], state_p)
    state_n, state_p = lax.optimization_barrier((state_n, state_p))
    state_n = attend(flags, q_own, [pair_up, pair_down, far_n], [0, 1, 5], state_n)
    state_p, state_n = lax.optimization_barrier((state_p, state_n))
    backs = []
    for part in (0, 1):
        out_p = attend(
            flags, q_pair, [(far_p_rows, 0), (far_p_rows, 1)], [3, 4], state_p, last=True, part=part
        )
        state_p, state_n, out_p = lax.optimization_barrier((state_p, state_n, out_p))
        backs.append(lax.ppermute(out_p, "ha", swap_pairs))
    out_n = attend(flags, q_own, [far_n_up, far_n_down], [6, 7], state_n, last=True)
    back_0, back_1, out_n = lax.optimization_barrier((*backs, out_n))

    core_pairs = [(i, i ^ 1) for i in range(4)]
    hi_pairs = [(i, i ^ 2) for i in range(4)]

    attention = jnp.concatenate([out_n, jnp.concatenate([back_0, back_1], axis=0)], axis=1)

    def partial_of(group, start, stop):
        return jnp.dot(attention[start:stop], weights[group], preferred_element_type=jnp.float32)

    fars = []
    for start in (0, tokens // 2):
        stop = start + tokens // 2
        taken = lax.ppermute(partial_of(0, start, stop).astype(jnp.bfloat16), "ta", core_pairs)
        away = (partial_of(1, start, stop) + taken.astype(jnp.float32)).astype(jnp.bfloat16)
        fars.append(lax.ppermute(away, "ta", hi_pairs))
    home_taken = lax.ppermute(partial_of(2, 0, tokens).astype(jnp.bfloat16), "ta", core_pairs)
    home = partial_of(3, 0, tokens) + home_taken.astype(jnp.float32)
    result = home + jnp.concatenate(fars, axis=0).astype(jnp.float32)
    return result.astype(jnp.bfloat16).reshape(frames, rows, cols, width)


def solution(mesh):
    return jax.shard_map(
        body,
        mesh=mesh,
        in_specs=(P(None, "wa", "ha", "ta"), P(None, None, "wa", "ha", "ta"), P("ta", None)),
        out_specs=P(None, "wa", "ha", "ta"),
        check_vma=False,
    )
```

```python
import functools

import jax
import jax.numpy as jnp
from jax import lax
from jax.experimental import pallas as pl
from jax.experimental.pallas import tpu as pltpu
from jax.sharding import PartitionSpec as P

HD = 128
LOG2E = 1.4426950408889634
EXP_SCALE = HD ** (-0.5) * LOG2E
LOW = -1e30
LIMIT = 2.0**60
KEYS = 256


COST2 = 1024
COST3 = 32


def attend_kernel(gates, first, last, step, *refs):
    flags_ref, q_ref = refs[:2]
    tiles = refs[2 : 2 + len(gates)]
    rest = refs[2 + len(gates) :]
    if not first:
        acc_in, top_in = rest[:2]
        rest = rest[2:]
    tokens = q_ref.shape[0]
    span = tiles[0].shape[1]
    inside = [None if gate is None else flags_ref[gate] > 0 for gate in gates]
    ones = jnp.ones((span, HD), jnp.bfloat16)

    def scores_of(queries, tile, begin, size):
        return lax.dot_general(
            queries, tile[0, pl.ds(begin, size), :], (((1,), (1,)), ((), ())),
            preferred_element_type=jnp.float32,
        )

    def row_max(scores):
        return jnp.broadcast_to(jnp.max(scores, axis=1, keepdims=True), (scores.shape[0], HD))

    def weights_of(scores, shift):
        wide = jnp.concatenate([shift] * (scores.shape[1] // HD), axis=1)
        return jnp.exp2((scores - wide) * EXP_SCALE).astype(jnp.bfloat16)

    def store(rows, mixed, top):
        if last:
            rest[0][rows, :] = (mixed[:, :HD] / mixed[:, HD:]).astype(rest[0].dtype)
        else:
            rest[0][rows, :] = mixed
            rest[1][rows, :] = top

    def full_step(start, all_scores):
        rows = pl.ds(start, step)
        old = jnp.full((step, HD), LOW, jnp.float32) if first else top_in[rows, :]
        new = old
        for scores, valid in zip(all_scores, inside):
            largest = row_max(scores)
            new = jnp.maximum(new, largest if valid is None else jnp.where(valid, largest, LOW))
        mixed = None
        for scores, valid, tile in zip(all_scores, inside, tiles):
            weights = weights_of(scores, new if valid is None else jnp.where(valid, new, -LOW))
            values = jnp.concatenate([tile[1], ones], axis=1)
            part = jnp.dot(weights, values, preferred_element_type=jnp.float32)
            mixed = part if mixed is None else mixed + part
        if not first:
            keep = jnp.exp2((old - new) * EXP_SCALE)
            mixed = acc_in[rows, :] * jnp.concatenate([keep, keep], axis=1) + mixed
        store(rows, mixed, new)

    def tile_scores(start):
        queries = q_ref[pl.ds(start, step), :]
        return [scores_of(queries, tile, 0, span) for tile in tiles]

    if first:
        ready = tile_scores(0)
        for start in range(0, tokens, step):
            following = tile_scores(start + step) if start + step < tokens else None
            full_step(start, ready)
            ready = following
        return

    def quick_weights(start):
        rows = pl.ds(start, step)
        queries = q_ref[rows, :]
        top = top_in[rows, :]
        parts = []
        for tile, valid in zip(tiles, inside):
            shift = top if valid is None else jnp.where(valid, top, -LOW)
            for begin in range(0, span, KEYS):
                parts.append(weights_of(scores_of(queries, tile, begin, KEYS), shift))
        return jnp.concatenate(parts, axis=1), top

    values = jnp.concatenate([jnp.concatenate([tile[1], ones], axis=1) for tile in tiles], axis=0)
    totals = None
    ready = quick_weights(0)
    for start in range(0, tokens, step):
        following = quick_weights(start + step) if start + step < tokens else None
        rows = pl.ds(start, step)
        mixed = jnp.dot(ready[0], values, preferred_element_type=jnp.float32)
        total = mixed[:, HD:]
        totals = total if totals is None else jnp.maximum(totals, total)
        store(rows, acc_in[rows, :] + mixed, ready[1])
        ready = following

    @pl.when(jnp.logical_not(jnp.max(totals) < LIMIT))
    def _():
        @pl.loop(0, tokens // step)
        def _(index):
            start = pl.multiple_of(index * step, step)
            full_step(start, tile_scores(start))


def attend(flags, queries, tiles, gates, state=None, last=False, part=None, cost=32):
    channels = queries.shape[1]
    tokens = queries.shape[0] if part is None else queries.shape[0] // 2
    heads = channels // HD
    span = queries.shape[0]
    arrays = [tile[0] if isinstance(tile, tuple) else tile for tile in tiles]

    def tile_spec(tile):
        if isinstance(tile, tuple):
            return pl.BlockSpec((None, 2, span, HD), lambda h: (tile[1], 0, 0, h))
        return pl.BlockSpec((2, span, HD), lambda h: (0, 0, h))

    def rows_spec(array, width):
        block = 0 if part is None or array.shape[0] == tokens else part
        return pl.BlockSpec((tokens, width), lambda h: (block, h))

    in_specs = [pl.BlockSpec(memory_space=pltpu.SMEM), rows_spec(queries, HD)] + [tile_spec(tile) for tile in tiles]
    args = [flags, queries, *arrays]
    if state is not None:
        in_specs += [rows_spec(state[0], 2 * HD), rows_spec(state[1], HD)]
        args += list(state)
    if last:
        out_shape = jax.ShapeDtypeStruct((tokens, channels), jnp.bfloat16)
        out_specs = rows_spec(out_shape, HD)
    else:
        out_shape = [
            jax.ShapeDtypeStruct((tokens, 2 * channels), jnp.float32),
            jax.ShapeDtypeStruct((tokens, channels), jnp.float32),
        ]
        out_specs = [rows_spec(out_shape[0], 2 * HD), rows_spec(out_shape[1], HD)]
    step = 256 if tokens % 256 == 0 else 192
    pairs = len(tiles) * heads * tokens * span
    return pl.pallas_call(
        functools.partial(attend_kernel, tuple(gates), state is None, last, step),
        out_shape=out_shape,
        grid=(heads,),
        in_specs=in_specs,
        out_specs=out_specs,
        compiler_params=pltpu.CompilerParams(vmem_limit_bytes=28 * 1024 * 1024),
        cost_estimate=pl.CostEstimate(flops=pairs * cost, bytes_accessed=1024, transcendentals=0),
    )(*args)


def body(queries, keys_values, out_weight):
    frames, rows, cols, channels = queries.shape
    tokens = frames * rows * cols
    half = channels // 2
    ha_count, wa_count = lax.axis_size("ha"), lax.axis_size("wa")
    ha, wa, ta = lax.axis_index("ha"), lax.axis_index("wa"), lax.axis_index("ta")
    odd = lax.rem(ha, 2)

    q_all = queries.reshape(tokens, channels)
    kv_all = keys_values.reshape(2, tokens, channels)
    keep_at, send_at = odd * half, (1 - odd) * half

    swap_pairs = [(i, i ^ 1) for i in range(ha_count)]
    native_pairs = [(i, (i + (2 if i % 2 else -2)) % ha_count) for i in range(ha_count)]
    swapped_pairs = [(i, (i + (-2 if i % 2 else 2)) % ha_count) for i in range(ha_count)]
    down_pairs = [(i, (i + 1) % wa_count) for i in range(wa_count)]
    up_pairs = [((i + 1) % wa_count, i) for i in range(wa_count)]

    def above_below(cells):
        return lax.ppermute(cells, "wa", down_pairs), lax.ppermute(cells, "wa", up_pairs)

    above, below = wa > 0, wa < wa_count - 1
    low, high = ha >= 2, ha < ha_count - 2
    far_partner = jnp.where(odd == 1, low, high)
    far_native = jnp.where(odd == 1, high, low)
    flags = jnp.stack(
        [above, below, far_partner, far_partner & above, far_partner & below,
         far_native, far_native & above, far_native & below]
    ).astype(jnp.int32)

    kv_send = lax.dynamic_slice_in_dim(kv_all, send_at, half, 2)
    kv_send, kv_all = lax.optimization_barrier((kv_send, kv_all))
    kv_own = lax.dynamic_slice_in_dim(kv_all, keep_at, half, 2)
    q_send = lax.dynamic_slice_in_dim(q_all, send_at, half, 1)
    q_own = lax.dynamic_slice_in_dim(q_all, keep_at, half, 1)

    core, x_hi = lax.rem(ta, 2), ta // 2
    width = out_weight.shape[1] // lax.axis_size("ta")
    ordered = jnp.concatenate(
        [lax.dynamic_slice_in_dim(out_weight, at, half, 0) for at in (keep_at, send_at)], axis=0
    )
    groups = (2 * (1 - x_hi) + 1 - core, 2 * (1 - x_hi) + core, 2 * x_hi + 1 - core, ta)
    weights = [lax.dynamic_slice_in_dim(ordered, group * width, width, 1) for group in groups]

    kv_pair = lax.ppermute(kv_send, "ha", swap_pairs)
    own_up, own_down = above_below(kv_own)
    far_p = lax.ppermute(kv_own, "ha", native_pairs)
    flags, *weights = lax.optimization_barrier((flags, *weights))
    state_n = attend(flags, q_own, [kv_own], [None])
    own_up, own_down, state_n = lax.optimization_barrier((own_up, own_down, state_n))
    far_p_rows = lax.ppermute(jnp.stack([own_up, own_down]), "ha", native_pairs)
    kv_pair, q_send, state_n, far_p = lax.optimization_barrier((kv_pair, q_send, state_n, far_p))
    q_pair = lax.ppermute(q_send, "ha", swap_pairs)
    pair_up, pair_down = above_below(kv_pair)
    far_n = lax.ppermute(kv_pair, "ha", swapped_pairs)

    state_n = attend(flags, q_own, [kv_pair, own_up, own_down], [None, 0, 1], state_n)
    q_pair, state_n = lax.optimization_barrier((q_pair, state_n))
    state_p = attend(flags, q_pair, [kv_own, kv_pair, own_up, own_down, far_p], [None, None, 0, 1, 2], cost=COST3)
    far_n, state_p = lax.optimization_barrier((far_n, state_p))
    far_n_up, far_n_down = above_below(far_n)
    state_p = attend(flags, q_pair, [pair_up, pair_down], [0, 1], state_p)
    state_n, state_p = lax.optimization_barrier((state_n, state_p))
    state_n = attend(flags, q_own, [pair_up, pair_down, far_n], [0, 1, 5], state_n)
    state_p, state_n = lax.optimization_barrier((state_p, state_n))
    backs = []
    for part in (0, 1):
        out_p = attend(
            flags, q_pair, [(far_p_rows, 0), (far_p_rows, 1)], [3, 4], state_p, last=True, part=part
        )
        state_p, state_n, out_p = lax.optimization_barrier((state_p, state_n, out_p))
        backs.append(lax.ppermute(out_p, "ha", swap_pairs))
    out_n = attend(flags, q_own, [far_n_up, far_n_down], [6, 7], state_n, last=True)
    back_0, back_1, out_n = lax.optimization_barrier((*backs, out_n))

    core_pairs = [(i, i ^ 1) for i in range(4)]
    hi_pairs = [(i, i ^ 2) for i in range(4)]

    attention = jnp.concatenate([out_n, jnp.concatenate([back_0, back_1], axis=0)], axis=1)

    def partial_of(group, start, stop):
        return jnp.dot(attention[start:stop], weights[group], preferred_element_type=jnp.float32)

    fars = []
    for start in (0, tokens // 2):
        stop = start + tokens // 2
        taken = lax.ppermute(partial_of(0, start, stop).astype(jnp.bfloat16), "ta", core_pairs)
        away = (partial_of(1, start, stop) + taken.astype(jnp.float32)).astype(jnp.bfloat16)
        fars.append(lax.ppermute(away, "ta", hi_pairs))
    home_taken = lax.ppermute(partial_of(2, 0, tokens).astype(jnp.bfloat16), "ta", core_pairs)
    home = partial_of(3, 0, tokens) + home_taken.astype(jnp.float32)
    home, *fars = lax.optimization_barrier((home, *fars))
    result = home + jnp.concatenate(fars, axis=0).astype(jnp.float32)
    return result.astype(jnp.bfloat16).reshape(frames, rows, cols, width)


def solution(mesh):
    return jax.shard_map(
        body,
        mesh=mesh,
        in_specs=(P(None, "wa", "ha", "ta"), P(None, None, "wa", "ha", "ta"), P("ta", None)),
        out_specs=P(None, "wa", "ha", "ta"),
        check_vma=False,
    )
```

```python
import functools

import jax
import jax.numpy as jnp
from jax import lax
from jax.experimental import pallas as pl
from jax.experimental.pallas import tpu as pltpu
from jax.sharding import PartitionSpec as P

HD = 128
LOG2E = 1.4426950408889634
EXP_SCALE = HD ** (-0.5) * LOG2E
LOW = -1e30
LIMIT = 2.0**60
KEYS = 256


COST2 = 1024
COST3 = 32


def attend_kernel(gates, first, last, step, *refs):
    flags_ref, q_ref = refs[:2]
    tiles = refs[2 : 2 + len(gates)]
    rest = refs[2 + len(gates) :]
    if not first:
        acc_in, top_in = rest[:2]
        rest = rest[2:]
    tokens = q_ref.shape[0]
    span = tiles[0].shape[1]
    inside = [None if gate is None else flags_ref[gate] > 0 for gate in gates]
    ones = jnp.ones((span, HD), jnp.bfloat16)

    def scores_of(queries, tile, begin, size):
        return lax.dot_general(
            queries, tile[0, pl.ds(begin, size), :], (((1,), (1,)), ((), ())),
            preferred_element_type=jnp.float32,
        )

    def row_max(scores):
        return jnp.broadcast_to(jnp.max(scores, axis=1, keepdims=True), (scores.shape[0], HD))

    def weights_of(scores, shift):
        wide = jnp.concatenate([shift] * (scores.shape[1] // HD), axis=1)
        return jnp.exp2((scores - wide) * EXP_SCALE).astype(jnp.bfloat16)

    def store(rows, mixed, top):
        if last:
            rest[0][rows, :] = (mixed[:, :HD] / mixed[:, HD:]).astype(rest[0].dtype)
        else:
            rest[0][rows, :] = mixed
            rest[1][rows, :] = top

    def full_step(start, all_scores):
        rows = pl.ds(start, step)
        old = jnp.full((step, HD), LOW, jnp.float32) if first else top_in[rows, :]
        new = old
        for scores, valid in zip(all_scores, inside):
            largest = row_max(scores)
            new = jnp.maximum(new, largest if valid is None else jnp.where(valid, largest, LOW))
        mixed = None
        for scores, valid, tile in zip(all_scores, inside, tiles):
            weights = weights_of(scores, new if valid is None else jnp.where(valid, new, -LOW))
            values = jnp.concatenate([tile[1], ones], axis=1)
            part = jnp.dot(weights, values, preferred_element_type=jnp.float32)
            mixed = part if mixed is None else mixed + part
        if not first:
            keep = jnp.exp2((old - new) * EXP_SCALE)
            mixed = acc_in[rows, :] * jnp.concatenate([keep, keep], axis=1) + mixed
        store(rows, mixed, new)

    def tile_scores(start):
        queries = q_ref[pl.ds(start, step), :]
        return [scores_of(queries, tile, 0, span) for tile in tiles]

    if first:
        ready = tile_scores(0)
        for start in range(0, tokens, step):
            following = tile_scores(start + step) if start + step < tokens else None
            full_step(start, ready)
            ready = following
        return

    def quick_weights(start):
        rows = pl.ds(start, step)
        queries = q_ref[rows, :]
        top = top_in[rows, :]
        parts = []
        for tile, valid in zip(tiles, inside):
            shift = top if valid is None else jnp.where(valid, top, -LOW)
            for begin in range(0, span, KEYS):
                parts.append(weights_of(scores_of(queries, tile, begin, KEYS), shift))
        return jnp.concatenate(parts, axis=1), top

    values = jnp.concatenate([jnp.concatenate([tile[1], ones], axis=1) for tile in tiles], axis=0)
    totals = None
    ready = quick_weights(0)
    for start in range(0, tokens, step):
        following = quick_weights(start + step) if start + step < tokens else None
        rows = pl.ds(start, step)
        mixed = jnp.dot(ready[0], values, preferred_element_type=jnp.float32)
        total = mixed[:, HD:]
        totals = total if totals is None else jnp.maximum(totals, total)
        store(rows, acc_in[rows, :] + mixed, ready[1])
        ready = following

    @pl.when(jnp.logical_not(jnp.max(totals) < LIMIT))
    def _():
        @pl.loop(0, tokens // step)
        def _(index):
            start = pl.multiple_of(index * step, step)
            full_step(start, tile_scores(start))


def attend(flags, queries, tiles, gates, state=None, last=False, part=None, cost=32):
    channels = queries.shape[1]
    tokens = queries.shape[0] if part is None else queries.shape[0] // 2
    heads = channels // HD
    span = queries.shape[0]
    arrays = [tile[0] if isinstance(tile, tuple) else tile for tile in tiles]

    def tile_spec(tile):
        if isinstance(tile, tuple):
            return pl.BlockSpec((None, 2, span, HD), lambda h: (tile[1], 0, 0, h))
        return pl.BlockSpec((2, span, HD), lambda h: (0, 0, h))

    def rows_spec(array, width):
        block = 0 if part is None or array.shape[0] == tokens else part
        return pl.BlockSpec((tokens, width), lambda h: (block, h))

    in_specs = [pl.BlockSpec(memory_space=pltpu.SMEM), rows_spec(queries, HD)] + [tile_spec(tile) for tile in tiles]
    args = [flags, queries, *arrays]
    if state is not None:
        in_specs += [rows_spec(state[0], 2 * HD), rows_spec(state[1], HD)]
        args += list(state)
    if last:
        out_shape = jax.ShapeDtypeStruct((tokens, channels), jnp.bfloat16)
        out_specs = rows_spec(out_shape, HD)
    else:
        out_shape = [
            jax.ShapeDtypeStruct((tokens, 2 * channels), jnp.float32),
            jax.ShapeDtypeStruct((tokens, channels), jnp.float32),
        ]
        out_specs = [rows_spec(out_shape[0], 2 * HD), rows_spec(out_shape[1], HD)]
    step = 256 if tokens % 256 == 0 else 192
    pairs = len(tiles) * heads * tokens * span
    return pl.pallas_call(
        functools.partial(attend_kernel, tuple(gates), state is None, last, step),
        out_shape=out_shape,
        grid=(heads,),
        in_specs=in_specs,
        out_specs=out_specs,
        compiler_params=pltpu.CompilerParams(vmem_limit_bytes=22 * 1024 * 1024),
        cost_estimate=pl.CostEstimate(flops=pairs * cost, bytes_accessed=1024, transcendentals=0),
    )(*args)


def body(queries, keys_values, out_weight):
    frames, rows, cols, channels = queries.shape
    tokens = frames * rows * cols
    half = channels // 2
    ha_count, wa_count = lax.axis_size("ha"), lax.axis_size("wa")
    ha, wa, ta = lax.axis_index("ha"), lax.axis_index("wa"), lax.axis_index("ta")
    odd = lax.rem(ha, 2)

    q_all = queries.reshape(tokens, channels)
    kv_all = keys_values.reshape(2, tokens, channels)
    keep_at, send_at = odd * half, (1 - odd) * half

    swap_pairs = [(i, i ^ 1) for i in range(ha_count)]
    native_pairs = [(i, (i + (2 if i % 2 else -2)) % ha_count) for i in range(ha_count)]
    swapped_pairs = [(i, (i + (-2 if i % 2 else 2)) % ha_count) for i in range(ha_count)]
    down_pairs = [(i, (i + 1) % wa_count) for i in range(wa_count)]
    up_pairs = [((i + 1) % wa_count, i) for i in range(wa_count)]

    def above_below(cells):
        return lax.ppermute(cells, "wa", down_pairs), lax.ppermute(cells, "wa", up_pairs)

    above, below = wa > 0, wa < wa_count - 1
    low, high = ha >= 2, ha < ha_count - 2
    far_partner = jnp.where(odd == 1, low, high)
    far_native = jnp.where(odd == 1, high, low)
    flags = jnp.stack(
        [above, below, far_partner, far_partner & above, far_partner & below,
         far_native, far_native & above, far_native & below]
    ).astype(jnp.int32)

    kv_send = lax.dynamic_slice_in_dim(kv_all, send_at, half, 2)
    kv_send, kv_all = lax.optimization_barrier((kv_send, kv_all))
    kv_own = lax.dynamic_slice_in_dim(kv_all, keep_at, half, 2)
    q_send = lax.dynamic_slice_in_dim(q_all, send_at, half, 1)
    q_own = lax.dynamic_slice_in_dim(q_all, keep_at, half, 1)

    core, x_hi = lax.rem(ta, 2), ta // 2
    width = out_weight.shape[1] // lax.axis_size("ta")
    ordered = jnp.concatenate(
        [lax.dynamic_slice_in_dim(out_weight, at, half, 0) for at in (keep_at, send_at)], axis=0
    )
    groups = (2 * (1 - x_hi) + 1 - core, 2 * (1 - x_hi) + core, 2 * x_hi + 1 - core, ta)
    weights = [lax.dynamic_slice_in_dim(ordered, group * width, width, 1) for group in groups]

    kv_pair = lax.ppermute(kv_send, "ha", swap_pairs)
    own_up, own_down = above_below(kv_own)
    far_p = lax.ppermute(kv_own, "ha", native_pairs)
    flags, *weights = lax.optimization_barrier((flags, *weights))
    state_n = attend(flags, q_own, [kv_own], [None])
    own_up, own_down, state_n = lax.optimization_barrier((own_up, own_down, state_n))
    far_p_rows = lax.ppermute(jnp.stack([own_up, own_down]), "ha", native_pairs)
    kv_pair, q_send, state_n, far_p = lax.optimization_barrier((kv_pair, q_send, state_n, far_p))
    q_pair = lax.ppermute(q_send, "ha", swap_pairs)
    pair_up, pair_down = above_below(kv_pair)
    far_n = lax.ppermute(kv_pair, "ha", swapped_pairs)

    state_n = attend(flags, q_own, [kv_pair, own_up, own_down], [None, 0, 1], state_n)
    q_pair, state_n = lax.optimization_barrier((q_pair, state_n))
    state_p = attend(flags, q_pair, [kv_own, kv_pair, own_up, own_down, far_p], [None, None, 0, 1, 2], cost=COST3)
    far_n, state_p = lax.optimization_barrier((far_n, state_p))
    far_n_up, far_n_down = above_below(far_n)
    state_p = attend(flags, q_pair, [pair_up, pair_down], [0, 1], state_p)
    state_n, state_p = lax.optimization_barrier((state_n, state_p))
    state_n = attend(flags, q_own, [pair_up, pair_down, far_n], [0, 1, 5], state_n)
    state_p, state_n = lax.optimization_barrier((state_p, state_n))
    backs = []
    for part in (0, 1):
        out_p = attend(
            flags, q_pair, [(far_p_rows, 0), (far_p_rows, 1)], [3, 4], state_p, last=True, part=part
        )
        state_p, state_n, out_p = lax.optimization_barrier((state_p, state_n, out_p))
        backs.append(lax.ppermute(out_p, "ha", swap_pairs))
    out_n = attend(flags, q_own, [far_n_up, far_n_down], [6, 7], state_n, last=True)
    back_0, back_1, out_n = lax.optimization_barrier((*backs, out_n))

    core_pairs = [(i, i ^ 1) for i in range(4)]
    hi_pairs = [(i, i ^ 2) for i in range(4)]

    attention = jnp.concatenate([out_n, jnp.concatenate([back_0, back_1], axis=0)], axis=1)

    def partial_of(group, start, stop):
        return jnp.dot(attention[start:stop], weights[group], preferred_element_type=jnp.float32)

    fars = []
    for start in (0, tokens // 2):
        stop = start + tokens // 2
        taken = lax.ppermute(partial_of(0, start, stop).astype(jnp.bfloat16), "ta", core_pairs)
        away = (partial_of(1, start, stop) + taken.astype(jnp.float32)).astype(jnp.bfloat16)
        fars.append(lax.ppermute(away, "ta", hi_pairs))
    home_taken = lax.ppermute(partial_of(2, 0, tokens).astype(jnp.bfloat16), "ta", core_pairs)
    home = partial_of(3, 0, tokens) + home_taken.astype(jnp.float32)
    home, *fars = lax.optimization_barrier((home, *fars))
    result = home + jnp.concatenate(fars, axis=0).astype(jnp.float32)
    return result.astype(jnp.bfloat16).reshape(frames, rows, cols, width)


def solution(mesh):
    return jax.shard_map(
        body,
        mesh=mesh,
        in_specs=(P(None, "wa", "ha", "ta"), P(None, None, "wa", "ha", "ta"), P("ta", None)),
        out_specs=P(None, "wa", "ha", "ta"),
        check_vma=False,
    )
```
